32 devices in a mesh: dp: 8 (over z, core), expert: 4 (over y, x).
Axes of the slice: x: 2, y: 2, z: 4, core: 2. Of those that a mesh axis runs over, the one named last changes fastest.
Arguments:
- normed: bfloat16 [1024, 6144], P(('dp', 'expert')), may hold values from -6 to 6
- upstream: bfloat16 [1024, 6144], P(('dp', 'expert')), may hold values from -6 to 6
- expert_ids: int32 [1024, 4], P(('dp', 'expert')), may hold values from 0 to 15, all different within a row; in each aligned block of 32 rows (0 to 31, 32 to 63, ...) at most 9 rows name the same one
- router_weight: bfloat16 [6144, 16], replicated, may hold values from -0.078125 to 0.078125
- gate_weight: bfloat16 [16, 20, 6144], P('expert'), may hold values from -0.078125 to 0.078125
- up_weight: bfloat16 [16, 20, 6144], P('expert'), may hold values from -0.078125 to 0.078125
- down_weight: bfloat16 [16, 20, 6144], P('expert'), may hold values from -1.25 to 1.25
- saved_inputs: bfloat16 [8, 16, 4, 9, 6144], P('dp', 'expert'), may hold values from -6 to 6
Outputs:
- grad_normed: bfloat16 [1024, 6144], P(('dp', 'expert'))
- router_grad: float32 [6144, 16], replicated
- grad_gate: float32 [16, 20, 6144], P('expert', None, 'dp')
- grad_up: float32 [16, 20, 6144], P('expert', None, 'dp')
- grad_down: float32 [16, 20, 6144], P('expert', None, 'dp')
The draws below stay inside these ranges and needn't reach their ends.
Inputs may be any that keep to these rules, and one draw needn't show every extreme that they name: `expert_ids`: each token names 4 different experts. Among the tokens of one device no expert is named more than 9 times, a bound that some block reaches.
All inputs are finite; a program needn't handle non-finite values.
Results may differ from the reference program's by a relative error of at most 0.0064.
Values may be sent and summed in bfloat16 or wider, within the bound.
No kernel may reach another device: no remote copies, remote signals or barrier semaphores. Data moves between devices by JAX's collectives and lax.ppermute only.
A program may use at most 64 MiB of HBM per device.

```python
import math
import jax
import jax.numpy as jnp
import numpy as np
from jax import lax

D = 6144
EXPERTS = 16
TOPK = 4
HB = 20
TOK_DEV = 32
CAP = 9
EXP_DEV = 4
TOKENS = 1024
N_DP = 8
N_EXPERT = 4


def level_of(stream_key, dims, cuts, low, high):
    factor_of = 1.0
    for axis_at, parts in cuts:
        heights = jax.random.uniform(jax.random.fold_in(jax.random.fold_in(stream_key, 6), axis_at), (parts,), jnp.float32, low / len(cuts), high / len(cuts))
        factor_of = factor_of * jnp.repeat(jnp.exp(heights), dims[axis_at] // parts).reshape((-1,) + (1,) * (len(dims) - 1 - axis_at))
    return factor_of


def assign_block(own_key, own, number, rows, number_of, top, bound, skew):
    sequence = jax.random.permutation(own_key, number_of)
    crowded, common = shares(number_of, rows * top, bound, skew, True), shares(number_of, rows * top, bound, skew, False)
    places = jnp.arange(number_of)

    def named(lengths, turn):
        used = int((lengths > 0).sum())
        fixed = max(1, used // 4)
        moved = fixed + (places - fixed + turn * (used - fixed)) % max(1, number_of - fixed)
        return jnp.zeros((number_of,), jnp.int32).at[sequence[jnp.where(places < fixed, places, moved)]].set(jnp.asarray(lengths, jnp.int32))

    lengths = jnp.where(number % 4 == 0, named(crowded, number // 4), named(common, number - number // 4 - 1))
    mixed = jax.random.permutation(jax.random.fold_in(own, 3), number_of)
    giver, taker = mixed[0:number_of // 2 * 2:2], mixed[1:number_of // 2 * 2:2]
    slack = jnp.minimum(lengths[giver] - 1, bound - lengths[taker]) // 2
    slack = jnp.where((giver == sequence[0]) | (taker == sequence[0]) | (lengths[taker] == 0), 0, jnp.maximum(slack, 0))
    moved = jax.random.randint(jax.random.fold_in(own, 4), (number_of // 2,), 0, 1 << 20) % (slack + 1)
    lengths = lengths.at[giver].add(-moved).at[taker].add(moved)
    items = jnp.searchsorted(jnp.cumsum(lengths), jnp.arange(rows * top), side="right").astype(jnp.int32)
    listing = items.reshape(top, rows).T
    listing = listing[jax.random.permutation(jax.random.fold_in(own, 1), rows)]
    turn = jax.random.randint(jax.random.fold_in(own, 2), (rows, 1), 0, top)
    return jnp.take_along_axis(listing, (jnp.arange(top)[None, :] + turn) % top, axis=1)


def shares(amount, total, limit, lean, full):
    weights = [(1 << 20) // math.isqrt(standing ** lean) + 1 for standing in range(1, amount + 1)]
    largest = limit if full else min(limit, max(-(-total // amount), total * weights[0] // sum(weights)))
    least = 1 if total - largest >= amount - 1 else 0
    holding, spare = [largest] + [least] * (amount - 1), total - largest - least * (amount - 1)
    while spare > 0:
        free = [i for i in range(1, amount) if holding[i] < largest] or [i for i in range(1, amount) if holding[i] < limit]
        mass, left = sum([weights[i] for i in free]), spare
        for i in free:
            more = min(limit - holding[i], max(1, left * weights[i] // mass), spare)
            holding[i] = holding[i] + more
            spare = spare - more
    return np.array(holding)


def normal_values(rng, shape, spread, most, split=(), kind=jnp.bfloat16):
    result = jax.random.normal(rng, shape, jnp.float32) * spread
    if len(split) > 0:
        result = level_of(rng, shape, split, -0.22, 0.18) * result
    return jnp.clip(result, min=-most, max=most).astype(kind)


def setup_inputs(seed: int = 0) -> dict:
    seeds = jax.random.split(jax.random.key(seed), 9)
    normed = normal_values(seeds[0], (TOKENS, D), 1.0, 6.0, ((0, 32),))
    upstream = normal_values(seeds[1], (TOKENS, D), 1.0, 6.0, ((0, 32),))
    expert_ids_keys = jax.random.split(jax.random.fold_in(seeds[2], 1), TOKENS // TOK_DEV)
    expert_ids_turns = jax.random.permutation(jax.random.fold_in(seeds[2], 3), TOKENS // TOK_DEV)
    expert_ids = jax.vmap(lambda own, number: assign_block(jax.random.fold_in(seeds[2], 2), own, number, TOK_DEV, EXPERTS, TOPK, CAP, 2))(expert_ids_keys, expert_ids_turns).reshape((TOKENS, TOPK))
    router_weight = normal_values(seeds[3], (D, EXPERTS), D ** -0.5, 0.078125)
    gate_weight = normal_values(seeds[4], (EXPERTS, HB, D), D ** -0.5, 0.078125, ((0, 4),))
    up_weight = normal_values(seeds[5], (EXPERTS, HB, D), D ** -0.5, 0.078125, ((0, 4),))
    down_weight = normal_values(seeds[6], (EXPERTS, HB, D), HB ** -0.5, 1.25, ((0, 4),))
    saved_inputs = normal_values(seeds[7], (N_DP, EXPERTS, N_EXPERT, CAP, D), 1.0, 6.0, ((0, 8), (1, 4)))
    return dict(normed=normed, upstream=upstream, expert_ids=expert_ids, router_weight=router_weight, gate_weight=gate_weight, up_weight=up_weight, down_weight=down_weight, saved_inputs=saved_inputs)


def slot_index(ids):
    flat_ids = ids.reshape(-1)
    choose = (flat_ids[:, None] == jnp.arange(EXPERTS, dtype=jnp.int32)[None, :]).astype(jnp.int32)
    before = jnp.cumsum(choose, axis=0) - choose
    place = jnp.sum(before * choose, axis=1).astype(jnp.int32)
    local = flat_ids % EXP_DEV
    owner = flat_ids // EXP_DEV
    return ((local * N_EXPERT + owner) * CAP + place).astype(jnp.int32)


def source_front(normed_dev, upstream_dev, ids_dev, router_weight):
    logits = jnp.dot(normed_dev, router_weight, preferred_element_type=jnp.float32)
    chosen = jnp.take_along_axis(logits, ids_dev, axis=1)
    top_weights = jax.nn.softmax(chosen, axis=-1)
    scaled = (top_weights[:, :, None] * upstream_dev[:, None, :].astype(jnp.float32)).astype(jnp.bfloat16)
    target = slot_index(ids_dev)
    total_slots = EXP_DEV * N_EXPERT * CAP
    outgoing = jnp.zeros((total_slots, D), jnp.bfloat16).at[target].set(scaled.reshape(-1, D))
    return top_weights, target, outgoing


def expert_math(inputs, grads_in, gate_weight, up_weight, down_weight):
    f32 = jnp.float32
    inputs_f = inputs.astype(f32)
    grads_f = grads_in.astype(f32)
    pre_gate = jnp.einsum('erd,efd->erf', inputs_f, gate_weight.astype(f32))
    pre_up = jnp.einsum('erd,efd->erf', inputs_f, up_weight.astype(f32))
    logistic = jax.nn.sigmoid(pre_gate)
    activated = pre_gate * logistic
    hidden = (activated * pre_up).astype(jnp.bfloat16)
    output = jnp.einsum('erf,efd->erd', hidden.astype(f32), down_weight.astype(f32))
    score = jnp.sum(grads_f * output, axis=-1).astype(jnp.bfloat16)
    grad_hidden = jnp.einsum('erd,efd->erf', grads_f, down_weight.astype(f32))
    slope = logistic * (1.0 + pre_gate * (1.0 - logistic))
    grad_pre_gate = (grad_hidden * pre_up * slope).astype(jnp.bfloat16)
    grad_pre_up = (grad_hidden * activated).astype(jnp.bfloat16)
    row_grad = (jnp.einsum('erf,efd->erd', grad_pre_gate.astype(f32), gate_weight.astype(f32))
                + jnp.einsum('erf,efd->erd', grad_pre_up.astype(f32), up_weight.astype(f32))).astype(jnp.bfloat16)
    term_gate = jnp.einsum('erf,erd->efd', grad_pre_gate.astype(f32), inputs_f)
    term_up = jnp.einsum('erf,erd->efd', grad_pre_up.astype(f32), inputs_f)
    term_down = jnp.einsum('erf,erd->efd', hidden.astype(f32), grads_f)
    return score, row_grad, term_gate, term_up, term_down


def reference(normed, upstream, expert_ids, router_weight, gate_weight, up_weight, down_weight, saved_inputs):
    f32 = jnp.float32
    normed_r = normed.reshape(N_DP, N_EXPERT, TOK_DEV, D)
    upstream_r = upstream.reshape(N_DP, N_EXPERT, TOK_DEV, D)
    ids_r = expert_ids.reshape(N_DP, N_EXPERT, TOK_DEV, TOPK)
    rows = N_EXPERT * CAP

    def one_replica(carry, pieces):
        acc_gate, acc_up, acc_down, acc_router = carry
        normed_i, upstream_i, ids_i, saved_i = pieces
        top_weights, target, outgoing = jax.vmap(source_front, in_axes=(0, 0, 0, None))(normed_i, upstream_i, ids_i, router_weight)
        arranged = outgoing.reshape(N_EXPERT, EXP_DEV, N_EXPERT, CAP, D).transpose(2, 1, 0, 3, 4).reshape(EXPERTS, rows, D)
        inputs = saved_i.reshape(EXPERTS, rows, D)
        score, row_grad, term_gate, term_up, term_down = expert_math(inputs, arranged, gate_weight, up_weight, down_weight)
        back_rows = row_grad.reshape(N_EXPERT, EXP_DEV, N_EXPERT, CAP, D).transpose(2, 1, 0, 3, 4).reshape(N_EXPERT, -1, D)
        back_scores = score.reshape(N_EXPERT, EXP_DEV, N_EXPERT, CAP).transpose(2, 1, 0, 3).reshape(N_EXPERT, -1)

        def source_back(normed_dev, ids_dev, weights_dev, target_dev, rows_dev, scores_dev):
            picked_rows = rows_dev[target_dev].astype(f32).reshape(TOK_DEV, TOPK, D)
            expert_grad = jnp.sum(picked_rows, axis=1)
            picked = scores_dev[target_dev].astype(f32).reshape(TOK_DEV, TOPK)
            grad_top = picked - weights_dev * jnp.sum(picked, axis=1, keepdims=True)
            hot = (ids_dev[:, :, None] == jnp.arange(EXPERTS, dtype=jnp.int32)[None, None, :]).astype(f32)
            grad_logits = jnp.sum(hot * grad_top[:, :, None], axis=1)
            router_term = jnp.dot(normed_dev.astype(f32).T, grad_logits, precision=lax.Precision.HIGHEST)
            through = jnp.dot(grad_logits, router_weight.astype(f32).T, precision=lax.Precision.HIGHEST)
            return (expert_grad + through).astype(jnp.bfloat16), router_term

        grad_i, router_terms = jax.vmap(source_back)(normed_i, ids_i, top_weights, target, back_rows, back_scores)
        carry = (acc_gate + term_gate, acc_up + term_up, acc_down + term_down, acc_router + jnp.sum(router_terms, axis=0))
        return carry, grad_i

    zeros_w = jnp.zeros((EXPERTS, HB, D), f32)
    start = (zeros_w, zeros_w, zeros_w, jnp.zeros((D, EXPERTS), f32))
    final, grads = lax.scan(one_replica, start, (normed_r, upstream_r, ids_r, saved_inputs))
    grad_gate, grad_up, grad_down, router_grad = final
    return grads.reshape(TOKENS, D), router_grad, grad_gate, grad_up, grad_down
```

```python
import functools

import jax
import jax.numpy as jnp
from jax import lax
from jax.experimental import pallas as pl
from jax.experimental.pallas import tpu as pltpu
from jax.sharding import PartitionSpec as P

F32 = jnp.float32
BF16 = jnp.bfloat16
LANES = 128
VMEM_BYTES = 48 * 2**20
HIGHEST = lax.Precision.HIGHEST


def dot(left, right, contract, precision=None):
    return lax.dot_general(
        left,
        right,
        ((contract[:1], contract[1:]), ((), ())),
        precision=precision,
        preferred_element_type=F32,
    )


def iota(shape, dim):
    return lax.broadcasted_iota(jnp.int32, shape, dim)


def whole(count):
    return [pl.BlockSpec(memory_space=pltpu.VMEM)] * count


def params(**more):
    return pltpu.CompilerParams(vmem_limit_bytes=VMEM_BYTES, **more)


def split_high_low(value):
    high = value.astype(BF16)
    return high, (value - high.astype(F32)).astype(BF16)


def route_kernel(experts, normed, router, ids, packed):
    tokens = normed.shape[0]
    logits = dot(normed[...], router[...], (1, 1))
    lane = iota((tokens, experts), 1)
    named = lane < 0
    for k in range(ids.shape[1]):
        named = named | (ids[:, k : k + 1] == lane)
    earlier = (iota((tokens, tokens), 1) < iota((tokens, tokens), 0)).astype(BF16)
    slot = dot(earlier, named.astype(F32).astype(BF16), (1, 0))
    largest = jnp.max(jnp.where(named, logits, -jnp.inf), axis=1, keepdims=True)
    weight = jnp.where(named, jnp.exp(jnp.where(named, logits - largest, 0.0)), 0.0)
    weight = weight / jnp.sum(weight, axis=1, keepdims=True)
    code = jnp.where(named, slot + 1.0, 0.0)
    packed[...] = jnp.concatenate(
        [weight, code, jnp.zeros((tokens, LANES - 2 * experts), F32)], axis=1
    )


def expert_kernel(sizes, me, *refs):
    n_expert, exp_dev, capacity, tokens_here = sizes
    rows_u, packs, rest = refs[:n_expert], refs[n_expert : 2 * n_expert], refs[2 * n_expert :]
    down, pre_gate, pre_up = rest[:3]
    scores = rest[3 : 3 + n_expert]
    tok_gate, tok_up, tok_hidden, slot_gate, slot_up = rest[3 + n_expert :]
    me = me[0]
    experts = exp_dev * n_expert
    tokens = tokens_here * n_expert
    hidden_all = down.shape[0]
    slots = exp_dev * capacity * n_expert
    packed = jnp.concatenate([p[...] for p in packs], axis=0)
    arrived = jnp.concatenate([u[...] for u in rows_u], axis=0)
    grad_hidden_raw = dot(arrived, down[...], (1, 1))

    lane_of_slot = me * exp_dev + iota((LANES, slots), 1) // (capacity * n_expert)
    pick_weight = (iota((LANES, slots), 0) == lane_of_slot).astype(F32)
    pick_code = (iota((LANES, slots), 0) == lane_of_slot + experts).astype(F32)
    weight_at = dot(packed, pick_weight, (1, 0), HIGHEST)
    code_at = dot(packed, pick_code, (1, 0))
    column = iota((tokens, slots), 1)
    source = me ^ (iota((tokens, slots), 0) // tokens_here)
    slot_code = ((column // n_expert) % capacity + 1).astype(F32)
    chosen = (source == column % n_expert) & (jnp.abs(code_at - slot_code) < 0.5)
    place = chosen.astype(F32).astype(BF16)
    place_weight = jnp.where(chosen, weight_at, 0.0)

    grad_hidden = dot(place_weight, grad_hidden_raw, (0, 0), HIGHEST)
    same = iota((slots, hidden_all), 1) % exp_dev == iota((slots, hidden_all), 0) // (capacity * n_expert)
    v = pre_gate[...]
    logistic = jax.nn.sigmoid(v)
    activated = v * logistic
    hidden = jnp.where(same, activated * pre_up[...], 0.0).astype(BF16)
    slope = logistic * (1.0 + v * (1.0 - logistic))
    grad_gate = jnp.where(same, grad_hidden * pre_up[...] * slope, 0.0).astype(BF16)
    grad_up = jnp.where(same, grad_hidden * activated, 0.0).astype(BF16)
    score = jnp.sum(hidden.astype(F32) * grad_hidden, axis=1, keepdims=True)
    lane_of_row = me * exp_dev + iota((slots, LANES), 0) // (capacity * n_expert)
    score = jnp.where(iota((slots, LANES), 1) == lane_of_row, score, 0.0).astype(BF16)
    picked = dot(place, score, (1, 0)).astype(BF16)
    for r in range(n_expert):
        scores[r][...] = picked[r * tokens_here : (r + 1) * tokens_here]
    slot_gate[...] = grad_gate
    slot_up[...] = grad_up
    tok_gate[...] = dot(place, grad_gate, (1, 0)).astype(BF16)
    tok_up[...] = dot(place, grad_up, (1, 0)).astype(BF16)
    lane_of_hidden = me * exp_dev + iota((LANES, hidden_all), 1) % exp_dev
    pick_hidden = (iota((LANES, hidden_all), 0) == lane_of_hidden).astype(F32)
    weight_hidden = dot(packed, pick_hidden, (1, 0), HIGHEST)
    tok_hidden[...] = (dot(place, hidden, (1, 0)) * weight_hidden).astype(BF16)


def weight_kernel(n_expert, at, slot_gate, slot_up, tok_hidden, inputs, *refs):
    del at
    rows_u, out = refs[:n_expert], refs[n_expert]
    n = slot_gate.shape[1]
    arrived = jnp.concatenate([u[...] for u in rows_u], axis=0)
    out[0, :n] = dot(slot_gate[...], inputs[...], (0, 0)).astype(out.dtype)
    out[0, n : 2 * n] = dot(slot_up[...], inputs[...], (0, 0)).astype(out.dtype)
    out[0, 2 * n :] = dot(tok_hidden[...], arrived, (0, 0)).astype(out.dtype)


def row_kernel(n_expert, tok_gate, tok_up, gate, up, *outs):
    total = dot(tok_gate[...], gate[...], (1, 0)) + dot(tok_up[...], up[...], (1, 0))
    size = total.shape[0] // n_expert
    for r in range(n_expert):
        outs[r][...] = total[r * size : (r + 1) * size].astype(outs[r].dtype)


def add_kernel(mine, theirs, *outs):
    for r in range(len(outs)):
        outs[r][...] = (mine[r].astype(F32) + theirs[r].astype(F32)).astype(outs[r].dtype)


def sum_kernel(*refs):
    pieces, outs = refs[:-3], refs[-3:]
    total = pieces[0][...].astype(F32)
    for piece in pieces[1:]:
        total = total + piece[...].astype(F32)
    n = total.shape[0] // 3
    for k in range(3):
        outs[k][...] = total[k * n : (k + 1) * n]


def router_kernel(experts, n_expert, at, *refs):
    del at
    scores, (packed, normed, router, term, through) = refs[:n_expert], refs[n_expert:]
    picked = scores[0][...].astype(F32)
    for s in scores[1:]:
        picked = picked + s[...].astype(F32)
    picked = picked[:, :experts]
    weight, code = packed[:, :experts], packed[:, experts : 2 * experts]
    grad = jnp.where(code > 0.5, picked - weight * jnp.sum(picked, axis=1, keepdims=True), 0.0)
    high, low = split_high_low(grad)
    term[...] = dot(high, normed[...], (0, 0)) + dot(low, normed[...], (0, 0))
    through[...] = dot(high, router[...], (1, 0)) + dot(low, router[...], (1, 0))


def final_kernel(*refs):
    pieces, out = refs[:-1], refs[-1]
    total = pieces[0][...].astype(F32)
    for piece in pieces[1:]:
        total = total + piece[...].astype(F32)
    out[...] = total.astype(out.dtype)


def on_device(normed, upstream, expert_ids, router_weight, gate_weight, up_weight, down_weight, saved_inputs):
    n_expert = lax.axis_size("expert")
    n_dp = lax.axis_size("dp")
    n_chip = n_dp // 2
    me = lax.axis_index("expert")
    dp = lax.axis_index("dp")
    core = dp & 1
    chip = dp >> 1
    exp_dev, hidden_units, width = gate_weight.shape
    capacity = saved_inputs.shape[3]
    experts = exp_dev * n_expert
    tokens_here = normed.shape[0]
    tokens = tokens_here * n_expert
    slots = exp_dev * capacity * n_expert
    hidden_all = exp_dev * hidden_units
    piece = width // n_dp
    shape = jax.ShapeDtypeStruct

    def over_expert(value, k):
        return lax.ppermute(value, "expert", [(i, i ^ k) for i in range(n_expert)])

    def over_core(value):
        return lax.ppermute(value, "dp", [(i, i ^ 1) for i in range(n_dp)])

    def over_chip(value, k):
        return lax.ppermute(value, "dp", [(i, i ^ (2 * k)) for i in range(n_dp)])

    def flat(weight):
        return jnp.transpose(weight, (1, 0, 2)).reshape(hidden_all, width)

    rows_u = [upstream] + [over_expert(upstream, k) for k in range(1, n_expert)]
    router = router_weight.T
    packed = pl.pallas_call(
        functools.partial(route_kernel, experts),
        out_shape=shape((tokens_here, LANES), F32),
        in_specs=whole(3),
        out_specs=pl.BlockSpec(memory_space=pltpu.VMEM),
        compiler_params=params(),
        name="route",
    )(normed, router, expert_ids)
    packs = [packed] + [over_expert(packed, k) for k in range(1, n_expert)]

    inputs = jnp.transpose(saved_inputs[0], (0, 2, 1, 3)).reshape(slots, width)
    gate, up, down = flat(gate_weight), flat(up_weight), flat(down_weight)
    pre_gate = dot(inputs, gate, (1, 1))
    pre_up = dot(inputs, up, (1, 1))

    here = jnp.stack([me]).astype(jnp.int32)
    outs = pl.pallas_call(
        functools.partial(expert_kernel, (n_expert, exp_dev, capacity, tokens_here)),
        out_shape=[shape((tokens_here, LANES), BF16)] * n_expert
        + [shape((tokens, hidden_all), BF16)] * 3
        + [shape((slots, hidden_all), BF16)] * 2,
        in_specs=[pl.BlockSpec(memory_space=pltpu.SMEM)] + whole(2 * n_expert + 3),
        out_specs=whole(n_expert + 5),
        compiler_params=params(),
        name="experts",
    )(here, *rows_u, *packs, down, pre_gate, pre_up)
    scores = outs[:n_expert]
    tok_gate, tok_up, tok_hidden, slot_gate, slot_up = outs[n_expert:]

    def weight_terms(owner_core, dtype):
        if piece % LANES:
            arrived = jnp.concatenate(rows_u, axis=0)
            terms = [dot(slot_gate, inputs, (0, 0)), dot(slot_up, inputs, (0, 0)), dot(tok_hidden, arrived, (0, 0))]
            terms = jnp.concatenate(terms, axis=0).reshape(3 * hidden_all, n_chip, 2, piece)
            terms = jnp.transpose(terms, (2, 1, 0, 3))[owner_core]
            return terms[chip ^ jnp.arange(n_chip)].astype(dtype)

        def block(r, at):
            return (0, 2 * (at[0] ^ r) + at[1])

        def same(r, at):
            return (0, 0)

        return pl.pallas_call(
            functools.partial(weight_kernel, n_expert),
            out_shape=shape((n_chip, 3 * hidden_all, piece), dtype),
            grid_spec=pltpu.PrefetchScalarGridSpec(
                num_scalar_prefetch=1,
                grid=(n_chip,),
                in_specs=[
                    pl.BlockSpec((slots, hidden_all), same),
                    pl.BlockSpec((slots, hidden_all), same),
                    pl.BlockSpec((tokens, hidden_all), same),
                    pl.BlockSpec((slots, piece), block),
                ]
                + [pl.BlockSpec((tokens_here, piece), block)] * n_expert,
                out_specs=pl.BlockSpec((1, 3 * hidden_all, piece), lambda r, at: (r, 0, 0)),
            ),
            compiler_params=params(),
            name="weight_terms",
        )(jnp.stack([chip, owner_core]).astype(jnp.int32), slot_gate, slot_up, tok_hidden, inputs, *rows_u)

    theirs = weight_terms(1 - core, BF16)
    from_core = over_core(theirs)
    mine = weight_terms(core, F32)

    row_pieces = pl.pallas_call(
        functools.partial(row_kernel, n_expert),
        out_shape=[shape((tokens_here, width), BF16)] * n_expert,
        grid=(8,),
        in_specs=[
            pl.BlockSpec((tokens, hidden_all), lambda j: (0, 0)),
            pl.BlockSpec((tokens, hidden_all), lambda j: (0, 0)),
            pl.BlockSpec((hidden_all, width // 8), lambda j: (0, j)),
            pl.BlockSpec((hidden_all, width // 8), lambda j: (0, j)),
        ],
        out_specs=[pl.BlockSpec((tokens_here, width // 8), lambda j: (0, j))] * n_expert,
        compiler_params=params(),
        name="row_terms",
    )(tok_gate, tok_up, gate, up)

    back_scores = [scores[0]] + [over_expert(scores[k], k) for k in range(1, n_expert)]
    back_rows = [row_pieces[0]] + [over_expert(row_pieces[k], k) for k in range(1, n_expert)]

    band = 3 * hidden_all if hidden_all % 16 else hidden_all
    chip_sums = pl.pallas_call(
        add_kernel,
        out_shape=[shape((3 * hidden_all, piece), F32)] + [shape((3 * hidden_all, piece), BF16)] * (n_chip - 1),
        grid=(3 * hidden_all // band,),
        in_specs=[pl.BlockSpec((n_chip, band, piece), lambda j: (0, j, 0))] * 2,
        out_specs=[pl.BlockSpec((band, piece), lambda j: (j, 0))] * n_chip,
        compiler_params=params(),
        name="core_sum",
    )(mine, from_core)
    chip_pieces = [chip_sums[0]] + [over_chip(chip_sums[k], k) for k in range(1, n_chip)]

    half = width // 2

    def parts(j, at):
        return (0, jnp.where(j == 0, 1 - at[0], at[0]))

    term, through = pl.pallas_call(
        functools.partial(router_kernel, experts, n_expert),
        out_shape=[shape((experts, width), F32), shape((tokens_here, width), F32)],
        grid_spec=pltpu.PrefetchScalarGridSpec(
            num_scalar_prefetch=1,
            grid=(2,),
            in_specs=[pl.BlockSpec((tokens_here, LANES), lambda j, at: (0, 0))] * (n_expert + 1)
            + [pl.BlockSpec((tokens_here, half), parts), pl.BlockSpec((experts, half), parts)],
            out_specs=[
                pl.BlockSpec((experts, half), lambda j, at: (0, j)),
                pl.BlockSpec((tokens_here, half), parts),
            ],
        ),
        compiler_params=params(),
        name="router_terms",
    )(jnp.stack([core]).astype(jnp.int32), *back_scores, packed, normed, router)
    total = term[:, half:] + over_core(term[:, :half])
    for k in range(n_expert.bit_length() - 1):
        low = total.astype(BF16)
        total = low.astype(F32) + over_expert(low, 1 << k).astype(F32)
    for k in range(n_chip.bit_length() - 1):
        low = total.astype(BF16)
        total = low.astype(F32) + over_chip(low, 1 << k).astype(F32)
    other = over_core(total)
    router_grad = jnp.where(
        core == 0, jnp.concatenate([total, other], axis=1), jnp.concatenate([other, total], axis=1)
    ).T

    grad_normed = pl.pallas_call(
        final_kernel,
        out_shape=shape((tokens_here, width), BF16),
        in_specs=whole(n_expert + 1),
        out_specs=pl.BlockSpec(memory_space=pltpu.VMEM),
        compiler_params=params(),
        name="grad_normed",
    )(through, *back_rows)
    grads = pl.pallas_call(
        sum_kernel,
        out_shape=[shape((hidden_all, piece), F32)] * 3,
        in_specs=whole(n_chip),
        out_specs=whole(3),
        compiler_params=params(),
        name="weight_sum",
    )(*chip_pieces)
    grads = [jnp.transpose(g.reshape(hidden_units, exp_dev, piece), (1, 0, 2)) for g in grads]
    return (grad_normed, router_grad, *grads)


def solution(mesh):
    placed = (
        P(("dp", "expert"), None),
        P(("dp", "expert"), None),
        P(("dp", "expert"), None),
        P(),
        P("expert", None, None),
        P("expert", None, None),
        P("expert", None, None),
        P("dp", "expert", None, None, None),
    )
    return jax.shard_map(
        on_device,
        mesh=mesh,
        in_specs=placed,
        out_specs=(
            P(("dp", "expert"), None),
            P(),
            P("expert", None, "dp"),
            P("expert", None, "dp"),
            P("expert", None, "dp"),
        ),
        check_vma=False,
    )
```

```python
import functools

import jax
import jax.numpy as jnp
from jax import lax
from jax.experimental import pallas as pl
from jax.experimental.pallas import tpu as pltpu
from jax.sharding import PartitionSpec as P

F32 = jnp.float32
BF16 = jnp.bfloat16
LANES = 128
TILE = 16
EARLY = 0
VMEM_BYTES = 16 * 2**20
HIGHEST = lax.Precision.HIGHEST


def dot(left, right, contract, precision=None):
    return lax.dot_general(
        left,
        right,
        ((contract[:1], contract[1:]), ((), ())),
        precision=precision,
        preferred_element_type=F32,
    )


def iota(shape, dim):
    return lax.broadcasted_iota(jnp.int32, shape, dim)


def split_high_low(value):
    high = value.astype(BF16)
    return high, (value - high.astype(F32)).astype(BF16)


def route_kernel(experts, ids, normed_hbm, router_hbm, upstream_hbm, packed, normed, router, upstream, sems):
    tokens, width = normed.shape
    copies = [
        pltpu.make_async_copy(source, target, sems.at[k])
        for k, (source, target) in enumerate(
            ((normed_hbm, normed), (router_hbm, router), (upstream_hbm, upstream))
        )
    ]
    for copy in copies:
        copy.start()
    expert = iota((experts, tokens), 0)
    named_t = expert < 0
    for k in range(ids.shape[0]):
        named_t = named_t | (ids[k : k + 1, :] == expert)
    unit = (iota((tokens, tokens), 0) == iota((tokens, tokens), 1)).astype(F32).astype(BF16)
    named_f = dot(unit, named_t.astype(F32).astype(BF16), (1, 1))
    named = named_f > 0.5
    earlier = (iota((tokens, tokens), 1) < iota((tokens, tokens), 0)).astype(F32).astype(BF16)
    slot = dot(earlier, named_f.astype(BF16), (1, 0))
    code = jnp.where(named, slot + 1.0, 0.0)
    copies[0].wait()
    copies[1].wait()
    logits = dot(normed[...], router[...], (1, 1))
    largest = jnp.max(jnp.where(named, logits, -jnp.inf), axis=1, keepdims=True)
    weight = jnp.where(named, jnp.exp(jnp.where(named, logits - largest, 0.0)), 0.0)
    weight = weight / jnp.sum(weight, axis=1, keepdims=True)
    high = weight.astype(BF16).astype(F32)
    middle = (weight - high).astype(BF16).astype(F32)
    low = weight - high - middle
    rest = jnp.zeros((tokens, LANES - 4 * experts), F32)
    packed[:, width:] = jnp.concatenate([high, middle, low, code, rest], axis=1).astype(BF16)
    copies[2].wait()
    packed[:, :width] = upstream[...]


def prepare_kernel(n_early, blocks, *refs):
    sources, refs = refs[:4], refs[4:]
    scratch, sems, refs = refs[-5:-1], refs[-1], refs[:-5]
    inputs, gate_rows, up_rows, down_rows, pre_gate, pre_up, *early = refs
    step = inputs.shape[1] // blocks
    copies = []
    for j in range(blocks):
        lanes = pl.ds(j * step, step)
        for k in range(4):
            copy = pltpu.make_async_copy(sources[k].at[:, :, lanes], scratch[k].at[:, :, lanes], sems.at[4 * j + k])
            copy.start()
            copies.append(copy)
    pre_gate[...] = jnp.zeros_like(pre_gate)
    pre_up[...] = jnp.zeros_like(pre_up)
    for j in range(blocks):
        lanes = slice(j * step, (j + 1) * step)
        for k, target in enumerate((inputs, gate_rows, up_rows, down_rows)):
            copies[4 * j + k].wait()
            target[:, lanes] = scratch[k][:, :, lanes].reshape(target.shape[0], step)
        pre_gate[...] += dot(inputs[:, lanes], gate_rows[:, lanes], (1, 1))
        pre_up[...] += dot(inputs[:, lanes], up_rows[:, lanes], (1, 1))
        if n_early:
            early[0][j] = inputs[: early[0].shape[1], lanes]


def pick(expert_of_column, experts, groups, columns):
    lane = iota((LANES, columns), 0)
    out = lane < 0
    for g in groups:
        out = out | (lane == expert_of_column + g * experts)
    return out.astype(F32).astype(BF16)


def unit_rows(rows, hidden_all, exp_dev, first, wanted):
    row, column = iota((rows, hidden_all), 0) - first, iota((rows, hidden_all), 1)
    return wanted(row, column // exp_dev, column % exp_dev).astype(F32).astype(BF16)


def block_terms(late, tok_hidden, inputs, rows_u, start, piece):
    at = pl.ds(pl.multiple_of(start, LANES), piece)
    arrived = jnp.concatenate([u[:, at] for u in rows_u], axis=0)
    return dot(late, inputs[:, at], (1, 0)), dot(tok_hidden, arrived, (1, 0))


def expert_kernel(sizes, at, *refs):
    n_expert, exp_dev, capacity, tokens_here, n_chip, piece, n_early = sizes
    rows_u, rest = refs[:n_expert], refs[n_expert:]
    down, pre_gate, pre_up, inputs = rest[:4]
    scores = rest[4 : 4 + n_expert]
    tok_gate, tok_up, tok_hidden, slot_late, slot_early = rest[4 + n_expert : 9 + n_expert]
    me, chip, core = at[0], at[1], at[2]
    experts = exp_dev * n_expert
    tokens = tokens_here * n_expert
    hidden_all, width = down.shape
    hidden_units = hidden_all // exp_dev
    slots = exp_dev * capacity * n_expert
    packed = jnp.concatenate([u[:, width:] for u in rows_u], axis=0)
    arrived = jnp.concatenate([u[:, :width] for u in rows_u], axis=0)
    grad_hidden_raw = dot(arrived, down[...], (1, 1))

    expert_of_slot = me * exp_dev + iota((LANES, slots), 1) // (capacity * n_expert)
    weight_at = dot(packed, pick(expert_of_slot, experts, (0, 1, 2), slots), (1, 0))
    code_at = dot(packed, pick(expert_of_slot, experts, (3,), slots), (1, 0))
    column = iota((tokens, slots), 1)
    source = me ^ (iota((tokens, slots), 0) // tokens_here)
    slot_code = ((column // n_expert) % capacity + 1).astype(F32)
    chosen = (source == column % n_expert) & (jnp.abs(code_at - slot_code) < 0.5)
    place = chosen.astype(F32).astype(BF16)
    place_weight = jnp.where(chosen, weight_at, 0.0)

    grad_hidden = dot(place_weight, grad_hidden_raw, (0, 0), HIGHEST)
    same = iota((slots, hidden_all), 1) % exp_dev == iota((slots, hidden_all), 0) // (capacity * n_expert)
    v = pre_gate[...]
    logistic = jax.nn.sigmoid(v)
    activated = v * logistic
    hidden = jnp.where(same, activated * pre_up[...], 0.0).astype(BF16)
    slope = logistic * (1.0 + v * (1.0 - logistic))
    grad_gate = jnp.where(same, grad_hidden * pre_up[...] * slope, 0.0).astype(BF16)
    grad_up = jnp.where(same, grad_hidden * activated, 0.0).astype(BF16)
    score = jnp.sum(hidden.astype(F32) * grad_hidden, axis=1, keepdims=True)
    expert_of_row = me * exp_dev + iota((slots, LANES), 0) // (capacity * n_expert)
    score = jnp.where(iota((slots, LANES), 1) == expert_of_row, score, 0.0)
    picked = dot(chosen.astype(F32), score, (1, 0), HIGHEST)
    for r in range(n_expert):
        scores[r][...] = picked[r * tokens_here : (r + 1) * tokens_here]
    tok_gate[...] = dot(place, grad_gate, (1, 0)).astype(BF16)
    tok_up[...] = dot(place, grad_up, (1, 0)).astype(BF16)
    expert_of_hidden = me * exp_dev + iota((LANES, hidden_all), 1) % exp_dev
    weight_hidden = dot(packed, pick(expert_of_hidden, experts, (0, 1, 2), hidden_all), (1, 0))
    scaled_hidden = (dot(place, hidden, (1, 0)) * weight_hidden).astype(BF16)
    n_late = exp_dev - n_early

    def pick_late(first):
        return unit_rows(
            slot_late.shape[0],
            hidden_all,
            exp_dev,
            first,
            lambda i, unit, e: (i >= 0) & (e >= n_early) & (i == (e - n_early) * hidden_units + unit),
        )

    late = dot(pick_late(0), grad_gate, (1, 1)) + dot(pick_late(n_late * hidden_units), grad_up, (1, 1))
    late = late.astype(BF16)
    order = unit_rows(hidden_all, hidden_all, exp_dev, 0, lambda i, unit, e: i == e * hidden_units + unit)
    turned = dot(order, scaled_hidden, (1, 1)).astype(BF16)
    slot_late[...], tok_hidden[...] = late, turned
    fold = [unit_rows(slot_early.shape[0], hidden_all, exp_dev, f, lambda i, unit, e: i == unit) for f in (0, hidden_units)]
    early = dot(fold[0], grad_gate, (1, 1)) + dot(fold[1], grad_up, (1, 1))
    slot_early[...] = early[:, :LANES].astype(BF16)
    if len(rest) > 9 + n_expert:
        theirs = rest[9 + n_expert]
        n = late.shape[0]
        for r in range(n_chip):
            start = (2 * (chip ^ r) + 1 - core) * piece
            first, second = block_terms(late, turned, inputs, rows_u, start, piece)
            theirs[r, :n] = first.astype(BF16)
            theirs[r, n:] = second.astype(BF16)


def weight_kernel(sizes, at, *refs):
    n_expert, n_chip, piece = sizes
    rows_u, (inputs, late, tok_hidden, mine) = refs[:n_expert], refs[n_expert:]
    chip, core = at[1], at[2]
    n = late.shape[0]
    for r in range(n_chip):
        start = (2 * (chip ^ r) + core) * piece
        first, second = block_terms(late[...], tok_hidden[...], inputs, rows_u, start, piece)
        mine[r, :n] = first
        mine[r, n:] = second


def add_kernel(n_early, mine, theirs, own, other, *refs):
    n_chip, m, _ = mine.shape
    outs = refs[-n_chip:]
    for r in range(n_chip):
        outs[r][:m] = (mine[r] + theirs[r].astype(F32)).astype(outs[r].dtype)
        if r and n_early:
            for k, lanes in enumerate(early_lanes(own.shape[0])):
                half = own if k < own.shape[0] // TILE else other
                block = k % (own.shape[0] // TILE)
                outs[r][m:, lanes] = half[block * TILE : (block + 1) * TILE]


def early_lanes(rows):
    return [slice(k * LANES, (k + 1) * LANES) for k in range(2 * rows // TILE)]


def row_kernel(n_expert, blocks, at, tok_gate, tok_up, gate, up, behind, out):
    del behind
    size = tok_gate.shape[0] // n_expert
    step = gate.shape[1] // blocks
    for j in range(blocks):
        lanes = slice(j * step, (j + 1) * step)
        total = dot(tok_gate[...], gate[:, lanes], (1, 0)) + dot(tok_up[...], up[:, lanes], (1, 0))
        for r in range(n_expert):
            out[at[0] ^ r, :, lanes] = total[r * size : (r + 1) * size].astype(out.dtype)


def sum_kernel(sizes, at, *refs):
    n_chip, exp_dev, hidden_units, slots_each, n_early = sizes
    pieces, own, other, rows = refs[:n_chip], refs[n_chip], refs[n_chip + 1], refs[n_chip + 2]
    outs = refs[-3:]
    chip, core = at[1], at[2]
    m = pieces[0].shape[0]
    n = m - exp_dev * hidden_units
    total = pieces[0][...]
    for piece in pieces[1:]:
        total = total + piece[:m].astype(F32)
    if n_early:
        count = n_early * hidden_units
        held, depth = own.shape[0], rows.shape[1]
        row, column = iota((2 * count, held), 0), iota((2 * count, held), 1)
        spread = (column == (row // count) * hidden_units + row % hidden_units).astype(F32).astype(BF16)
        same = (iota((2 * count, LANES), 0) % count) // hidden_units == iota((2 * count, LANES), 1) // slots_each
        early = jnp.zeros((2 * count, rows.shape[2]), F32)
        for r in range(n_chip):
            for c in range(2):
                if r:
                    half = early_lanes(held)[c * held // TILE : (c + 1) * held // TILE]
                    narrow = jnp.concatenate([pieces[r][m:, lanes] for lanes in half], axis=0)
                else:
                    narrow = (own, other)[c][...]
                wide = jnp.where(same, dot(spread, narrow, (1, 0)), 0.0).astype(BF16)
                early = early + dot(wide[:, :depth], rows[2 * (chip ^ r) + (core ^ c)], (1, 0))
    for k in range(2):
        for e in range(exp_dev):
            if e < n_early:
                first = (k * n_early + e) * hidden_units
                outs[k][:, e, :] = early[first : first + hidden_units]
            else:
                first = (k * (exp_dev - n_early) + e - n_early) * hidden_units
                outs[k][:, e, :] = total[first : first + hidden_units]
    for e in range(exp_dev):
        outs[2][:, e, :] = total[n + e * hidden_units : n + (e + 1) * hidden_units]


def router_kernel(experts, n_expert, at, *refs):
    scores, (packed, normed, router, other, own, through) = refs[:n_expert], refs[n_expert:]
    picked = scores[0][...]
    for s in scores[1:]:
        picked = picked + s[...]
    picked = picked[:, :experts]
    width = normed.shape[1]
    half = width // 2
    tail = packed[:, width:].astype(F32)
    weight = tail[:, :experts] + tail[:, experts : 2 * experts] + tail[:, 2 * experts : 3 * experts]
    code = tail[:, 3 * experts : 4 * experts]
    grad = jnp.where(code > 0.5, picked - weight * jnp.sum(picked, axis=1, keepdims=True), 0.0)
    high, low = split_high_low(grad)
    core = at[2]
    for out, part in ((other, 1 - core), (own, core)):
        values = normed[:, pl.ds(pl.multiple_of(part * half, LANES), half)]
        out[...] = dot(high, values, (0, 0)) + dot(low, values, (0, 0))
    through[...] = dot(high, router[...], (1, 0)) + dot(low, router[...], (1, 0))


def final_kernel(through, pieces, out):
    total = through[...]
    for r in range(pieces.shape[0]):
        total = total + pieces[r].astype(F32)
    out[...] = total.astype(out.dtype)


def on_device(normed, upstream, expert_ids, router_weight, gate_weight, up_weight, down_weight, saved_inputs):
    n_expert = lax.axis_size("expert")
    n_dp = lax.axis_size("dp")
    n_chip = n_dp // 2
    me = lax.axis_index("expert")
    dp = lax.axis_index("dp")
    core = dp & 1
    chip = dp >> 1
    exp_dev, hidden_units, width = gate_weight.shape
    capacity = saved_inputs.shape[3]
    experts = exp_dev * n_expert
    tokens_here = normed.shape[0]
    tokens = tokens_here * n_expert
    slots = exp_dev * capacity * n_expert
    hidden_all = exp_dev * hidden_units
    piece = width // n_dp
    half = width // 2
    even = piece % LANES == 0
    slots_each = capacity * n_expert
    narrow = -(-2 * hidden_units // TILE) * TILE
    n_early = EARLY * exp_dev // 4
    early_rows = -(-n_early * slots_each // TILE) * TILE
    if not even or early_rows > min(LANES, slots) or 2 * narrow // TILE * LANES > piece:
        n_early = 0
    late_rows = -(-2 * (exp_dev - n_early) * hidden_units // TILE) * TILE
    sent_rows = late_rows + hidden_all
    shape = jax.ShapeDtypeStruct

    def over_expert(value, k):
        return lax.ppermute(value, "expert", [(i, i ^ k) for i in range(n_expert)])

    def over_core(value):
        return lax.ppermute(value, "dp", [(i, i ^ 1) for i in range(n_dp)])

    def over_chip(value, k):
        return lax.ppermute(value, "dp", [(i, i ^ (2 * k)) for i in range(n_dp)])

    def call(kernel, name, outs, args, scalars=False, behind=0):
        specs = [pl.BlockSpec(memory_space=pltpu.VMEM)] * len(args)
        if scalars:
            specs[0] = pl.BlockSpec(memory_space=pltpu.SMEM)
        for k in range(behind):
            specs[-1 - k] = pl.BlockSpec(memory_space=pl.ANY)
        return pl.pallas_call(
            kernel,
            out_shape=outs,
            in_specs=specs,
            out_specs=[pl.BlockSpec(memory_space=pltpu.VMEM)] * len(outs),
            compiler_params=pltpu.CompilerParams(vmem_limit_bytes=VMEM_BYTES),
            cost_estimate=pl.CostEstimate(flops=0, bytes_accessed=0, transcendentals=0),
            name=name,
        )(*args)

    at = jnp.stack([me, chip, core]).astype(jnp.int32)
    router = router_weight.T
    packed = pl.pallas_call(
        functools.partial(route_kernel, experts),
        out_shape=shape((tokens_here, width + LANES), BF16),
        in_specs=[pl.BlockSpec(memory_space=pltpu.VMEM)] + [pl.BlockSpec(memory_space=pltpu.HBM)] * 3,
        out_specs=pl.BlockSpec(memory_space=pltpu.VMEM),
        scratch_shapes=[
            pltpu.VMEM((tokens_here, width), BF16),
            pltpu.VMEM((experts, width), BF16),
            pltpu.VMEM((tokens_here, width), BF16),
            pltpu.SemaphoreType.DMA((3,)),
        ],
        compiler_params=pltpu.CompilerParams(vmem_limit_bytes=VMEM_BYTES),
        cost_estimate=pl.CostEstimate(flops=0, bytes_accessed=0, transcendentals=0),
        name="route",
    )(expert_ids.T, normed, router, upstream)
    rows_u = [packed] + [over_expert(packed, k) for k in range(1, n_expert)]

    blocks = n_dp if even else 8
    sources = [jnp.transpose(saved_inputs[0], (0, 2, 1, 3)).reshape(exp_dev * capacity, n_expert, width)]
    sources += [jnp.transpose(w, (1, 0, 2)) for w in (gate_weight, up_weight, down_weight)]
    results = (
        [shape((slots, width), BF16)]
        + [shape((hidden_all, width), BF16)] * 3
        + [shape((slots, hidden_all), F32)] * 2
        + [shape((n_dp, early_rows, piece), BF16)] * bool(n_early)
    )
    inputs, gate, up, down, pre_gate, pre_up, *early_x = pl.pallas_call(
        functools.partial(prepare_kernel, n_early, blocks),
        out_shape=results,
        in_specs=[pl.BlockSpec(memory_space=pltpu.HBM)] * 4,
        out_specs=[pl.BlockSpec(memory_space=pltpu.VMEM)] * len(results),
        scratch_shapes=[pltpu.VMEM(source.shape, BF16) for source in sources]
        + [pltpu.SemaphoreType.DMA((4 * blocks,))],
        compiler_params=pltpu.CompilerParams(vmem_limit_bytes=VMEM_BYTES),
        cost_estimate=pl.CostEstimate(flops=0, bytes_accessed=0, transcendentals=0),
        name="prepare",
    )(*sources)
    if n_early:
        early_x = lax.all_to_all(early_x[0], "dp", 0, 0, tiled=True)

    outs = call(
        functools.partial(expert_kernel, (n_expert, exp_dev, capacity, tokens_here, n_chip, piece, n_early)),
        "experts",
        [shape((tokens_here, LANES), F32)] * n_expert
        + [shape((tokens, hidden_all), BF16)] * 2
        + [shape((hidden_all, tokens), BF16), shape((late_rows, slots), BF16), shape((narrow, LANES), BF16)]
        + [shape((n_chip, sent_rows, piece), BF16)] * even,
        (at, *rows_u, down, pre_gate, pre_up, inputs),
        scalars=True,
    )
    scores = outs[:n_expert]
    tok_gate, tok_up, tok_hidden, slot_late, own_narrow = outs[n_expert : n_expert + 5]
    back_scores = [scores[0]] + [over_expert(scores[k], k) for k in range(1, n_expert)]
    other_narrow = over_core(own_narrow) if n_early else own_narrow
    if even:
        from_core = over_core(outs[n_expert + 5])
        sent = shape((sent_rows + TILE * bool(n_early), piece), BF16)
        (mine,) = call(
            functools.partial(weight_kernel, (n_expert, n_chip, piece)),
            "weight_terms",
            [shape((n_chip, sent_rows, piece), F32)],
            (at, *rows_u, inputs, slot_late, tok_hidden),
            scalars=True,
        )
        chip_sums = call(
            functools.partial(add_kernel, n_early),
            "core_sum",
            [shape((sent_rows, piece), F32)] + [sent] * (n_chip - 1),
            (mine, from_core, own_narrow, other_narrow, *back_scores[1:]),
            behind=n_expert - 1,
        )
    else:
        arrived = jnp.concatenate([u[:, :width] for u in rows_u], axis=0)
        terms = [dot(slot_late, inputs, (1, 0)), dot(tok_hidden, arrived, (1, 0))]
        terms = jnp.concatenate(terms, axis=0).reshape(sent_rows, n_chip, 2, piece)
        terms = jnp.transpose(terms, (2, 1, 0, 3))
        from_core = over_core(terms[1 - core].astype(BF16))
        terms = terms[core] + from_core.astype(F32)
        chip_sums = [terms[chip ^ k].astype(BF16 if k else F32) for k in range(n_chip)]
    chip_pieces = [chip_sums[0]] + [over_chip(chip_sums[k], k) for k in range(1, n_chip)]

    always = expert_ids[0, 0] >= 0

    def sum_chips(total):
        for k in range(n_chip.bit_length() - 1):
            total = lax.reduce_precision(total, 8, 7)
            total = total + over_chip(total.astype(BF16), 1 << k).astype(F32)
        other = over_core(total)
        return jnp.where(
            core == 0, jnp.concatenate([total, other], axis=1), jnp.concatenate([other, total], axis=1)
        )

    def way_back(values):
        back_scores, packed, normed, router, tok_gate, tok_up, gate, up = values
        other, own, through = call(
            functools.partial(router_kernel, experts, n_expert),
            "router_terms",
            [shape((experts, half), F32)] * 2 + [shape((tokens_here, width), F32)],
            (at, *back_scores, packed, normed, router),
            scalars=True,
        )
        total = own + over_core(other)
        for k in range(n_expert.bit_length() - 1):
            total = lax.reduce_precision(total, 8, 7)
            total = total + over_expert(total.astype(BF16), 1 << k).astype(F32)
        (row_pieces,) = call(
            functools.partial(row_kernel, n_expert, 8),
            "row_terms",
            [shape((n_expert, tokens_here, width), BF16)],
            (at, tok_gate, tok_up, gate, up, total),
            scalars=True,
            behind=1,
        )
        back_rows = lax.all_to_all(row_pieces, "expert", 0, 0, tiled=True)
        total, _ = lax.optimization_barrier((total, row_pieces))
        router_grad = lax.cond(always, sum_chips, lambda total: jnp.concatenate([total, total], axis=1), total)
        (grad_normed,) = call(
            final_kernel, "grad_normed", [shape((tokens_here, width), BF16)], (through, back_rows)
        )
        return grad_normed, router_grad

    grad_normed, router_grad = lax.cond(
        always,
        way_back,
        lambda values: (jnp.zeros((tokens_here, width), BF16), jnp.zeros((experts, width), F32)),
        (back_scores, packed, normed, router, tok_gate, tok_up, gate, up),
    )
    if not n_early:
        early_x = jnp.zeros((TILE, LANES), BF16)
    grads = call(
        functools.partial(sum_kernel, (n_chip, exp_dev, hidden_units, slots_each, n_early)),
        "weight_sum",
        [shape((hidden_units, exp_dev, piece), F32)] * 3,
        (at, *chip_pieces, own_narrow, other_narrow, early_x, grad_normed, router_grad),
        scalars=True,
        behind=2,
    )
    grads = [jnp.transpose(g, (1, 0, 2)) for g in grads]
    return (grad_normed, router_grad.T, *grads)


def solution(mesh):
    placed = (
        P(("dp", "expert"), None),
        P(("dp", "expert"), None),
        P(("dp", "expert"), None),
        P(),
        P("expert", None, None),
        P("expert", None, None),
        P("expert", None, None),
        P("dp", "expert", None, None, None),
    )
    return jax.shard_map(
        on_device,
        mesh=mesh,
        in_specs=placed,
        out_specs=(
            P(("dp", "expert"), None),
            P(),
            P("expert", None, "dp"),
            P("expert", None, "dp"),
            P("expert", None, "dp"),
        ),
        check_vma=False,
    )
```

```python
import functools

import jax
import jax.numpy as jnp
from jax import lax
from jax.experimental import pallas as pl
from jax.experimental.pallas import tpu as pltpu
from jax.sharding import PartitionSpec as P

F32 = jnp.float32
BF16 = jnp.bfloat16
LANES = 128
TILE = 16
EARLY = 0
VMEM_BYTES = 16 * 2**20
HIGHEST = lax.Precision.HIGHEST


def dot(left, right, contract, precision=None):
    return lax.dot_general(
        left,
        right,
        ((contract[:1], contract[1:]), ((), ())),
        precision=precision,
        preferred_element_type=F32,
    )


def iota(shape, dim):
    return lax.broadcasted_iota(jnp.int32, shape, dim)


def split_high_low(value):
    high = value.astype(BF16)
    return high, (value - high.astype(F32)).astype(BF16)


def route_kernel(experts, *refs):
    sources, (first, packed, ids, normed, router, upstream, sems) = refs[:4], refs[4:]
    tokens, width = normed.shape
    half = width // 2
    copies = [
        pltpu.make_async_copy(source, target, sems.at[k])
        for k, (source, target) in enumerate(zip(sources, (ids, normed, router, upstream)))
    ]
    for copy in copies:
        copy.start()
    copies[0].wait()
    expert = iota((experts, tokens), 0)
    named_t = expert < 0
    for k in range(ids.shape[0]):
        named_t = named_t | (ids[k : k + 1, :] == expert)
    unit = (iota((tokens, tokens), 0) == iota((tokens, tokens), 1)).astype(F32).astype(BF16)
    named_f = dot(unit, named_t.astype(F32).astype(BF16), (1, 1))
    named = named_f > 0.5
    earlier = (iota((tokens, tokens), 1) < iota((tokens, tokens), 0)).astype(F32).astype(BF16)
    slot = dot(earlier, named_f.astype(BF16), (1, 0))
    code = jnp.where(named, slot + 1.0, 0.0)
    copies[1].wait()
    copies[2].wait()
    logits = dot(normed[...], router[...], (1, 1))
    largest = jnp.max(jnp.where(named, logits, -jnp.inf), axis=1, keepdims=True)
    weight = jnp.where(named, jnp.exp(jnp.where(named, logits - largest, 0.0)), 0.0)
    weight = weight / jnp.sum(weight, axis=1, keepdims=True)
    high = weight.astype(BF16).astype(F32)
    middle = (weight - high).astype(BF16).astype(F32)
    low = weight - high - middle
    rest = jnp.zeros((tokens, LANES - 4 * experts), F32)
    packed[:, half:] = jnp.concatenate([high, middle, low, code, rest], axis=1).astype(BF16)
    copies[3].wait()
    first[...] = upstream[:, :half]
    packed[:, :half] = upstream[:, half:]


def prepare_kernel(n_early, blocks, *refs):
    sources, refs = refs[:4], refs[4:]
    scratch, sems, refs = refs[-5:-1], refs[-1], refs[:-5]
    inputs, gate_rows, up_rows, down_rows, pre_gate, pre_up, *early = refs
    step = inputs.shape[1] // blocks
    copies = []
    for j in range(blocks):
        lanes = pl.ds(j * step, step)
        for k in range(4):
            copy = pltpu.make_async_copy(sources[k].at[:, :, lanes], scratch[k].at[:, :, lanes], sems.at[4 * j + k])
            copy.start()
            copies.append(copy)
    pre_gate[...] = jnp.zeros_like(pre_gate)
    pre_up[...] = jnp.zeros_like(pre_up)
    for j in range(blocks):
        lanes = slice(j * step, (j + 1) * step)
        for k, target in enumerate((inputs, gate_rows, up_rows, down_rows)):
            copies[4 * j + k].wait()
            target[:, lanes] = scratch[k][:, :, lanes].reshape(target.shape[0], step)
        pre_gate[...] += dot(inputs[:, lanes], gate_rows[:, lanes], (1, 1))
        pre_up[...] += dot(inputs[:, lanes], up_rows[:, lanes], (1, 1))
        if n_early:
            early[0][j] = inputs[: early[0].shape[1], lanes]


def pick(expert_of_column, experts, groups, columns):
    lane = iota((LANES, columns), 0)
    out = lane < 0
    for g in groups:
        out = out | (lane == expert_of_column + g * experts)
    return out.astype(F32).astype(BF16)


def unit_rows(rows, hidden_all, exp_dev, first, wanted):
    row, column = iota((rows, hidden_all), 0) - first, iota((rows, hidden_all), 1)
    return wanted(row, column // exp_dev, column % exp_dev).astype(F32).astype(BF16)


def block_terms(late, tok_hidden, inputs, arrived, start, piece):
    at = pl.ds(pl.multiple_of(start, LANES), piece)
    return dot(late, inputs[:, at], (1, 0)), dot(tok_hidden, arrived[:, at], (1, 0))


def expert_kernel(sizes, at, *refs):
    n_expert, exp_dev, capacity, tokens_here, n_chip, piece, n_early, even = sizes
    firsts, seconds, rest = refs[:n_expert], refs[n_expert : 2 * n_expert], refs[2 * n_expert :]
    down, pre_gate, pre_up, inputs = rest[:4]
    scores = rest[4 : 4 + n_expert]
    tok_gate, tok_up, tok_hidden, slot_late, slot_early, arrived = rest[4 + n_expert : 10 + n_expert]
    me, chip, core = at[0], at[1], at[2]
    experts = exp_dev * n_expert
    tokens = tokens_here * n_expert
    hidden_all, width = down.shape
    half = width // 2
    hidden_units = hidden_all // exp_dev
    slots = exp_dev * capacity * n_expert
    packed = jnp.concatenate([u[:, half:] for u in seconds], axis=0)
    for r in range(n_expert):
        rows = slice(r * tokens_here, (r + 1) * tokens_here)
        arrived[rows, :half] = firsts[r][...]
        arrived[rows, half:] = seconds[r][:, :half]
    grad_hidden_raw = dot(arrived[...], down[...], (1, 1))

    expert_of_slot = me * exp_dev + iota((LANES, slots), 1) // (capacity * n_expert)
    weight_at = dot(packed, pick(expert_of_slot, experts, (0, 1, 2), slots), (1, 0))
    code_at = dot(packed, pick(expert_of_slot, experts, (3,), slots), (1, 0))
    column = iota((tokens, slots), 1)
    source = me ^ (iota((tokens, slots), 0) // tokens_here)
    slot_code = ((column // n_expert) % capacity + 1).astype(F32)
    chosen = (source == column % n_expert) & (jnp.abs(code_at - slot_code) < 0.5)
    place = chosen.astype(F32).astype(BF16)
    place_weight = jnp.where(chosen, weight_at, 0.0)

    grad_hidden = dot(place_weight, grad_hidden_raw, (0, 0), HIGHEST)
    same = iota((slots, hidden_all), 1) % exp_dev == iota((slots, hidden_all), 0) // (capacity * n_expert)
    v = pre_gate[...]
    logistic = jax.nn.sigmoid(v)
    activated = v * logistic
    hidden = jnp.where(same, activated * pre_up[...], 0.0).astype(BF16)
    slope = logistic * (1.0 + v * (1.0 - logistic))
    grad_gate = jnp.where(same, grad_hidden * pre_up[...] * slope, 0.0).astype(BF16)
    grad_up = jnp.where(same, grad_hidden * activated, 0.0).astype(BF16)
    score = jnp.sum(hidden.astype(F32) * grad_hidden, axis=1, keepdims=True)
    expert_of_row = me * exp_dev + iota((slots, LANES), 0) // (capacity * n_expert)
    score = jnp.where(iota((slots, LANES), 1) == expert_of_row, score, 0.0)
    picked = dot(chosen.astype(F32), score, (1, 0), HIGHEST)
    for r in range(n_expert):
        scores[r][...] = picked[r * tokens_here : (r + 1) * tokens_here]
    tok_gate[...] = dot(place, grad_gate, (1, 0)).astype(BF16)
    tok_up[...] = dot(place, grad_up, (1, 0)).astype(BF16)
    expert_of_hidden = me * exp_dev + iota((LANES, hidden_all), 1) % exp_dev
    weight_hidden = dot(packed, pick(expert_of_hidden, experts, (0, 1, 2), hidden_all), (1, 0))
    scaled_hidden = (dot(place, hidden, (1, 0)) * weight_hidden).astype(BF16)
    n_late = exp_dev - n_early

    def pick_late(first):
        return unit_rows(
            slot_late.shape[0],
            hidden_all,
            exp_dev,
            first,
            lambda i, unit, e: (i >= 0) & (e >= n_early) & (i == (e - n_early) * hidden_units + unit),
        )

    late = dot(pick_late(0), grad_gate, (1, 1)) + dot(pick_late(n_late * hidden_units), grad_up, (1, 1))
    late = late.astype(BF16)
    order = unit_rows(hidden_all, hidden_all, exp_dev, 0, lambda i, unit, e: i == e * hidden_units + unit)
    turned = dot(order, scaled_hidden, (1, 1)).astype(BF16)
    slot_late[...], tok_hidden[...] = late, turned
    fold = [unit_rows(slot_early.shape[0], hidden_all, exp_dev, f, lambda i, unit, e: i == unit) for f in (0, hidden_units)]
    early = dot(fold[0], grad_gate, (1, 1)) + dot(fold[1], grad_up, (1, 1))
    slot_early[...] = early[:, :LANES].astype(BF16)
    if even:
        theirs = rest[10 + n_expert]
        n = late.shape[0]
        for r in range(n_chip):
            start = (2 * (chip ^ r) + 1 - core) * piece
            first, second = block_terms(late, turned, inputs, arrived, start, piece)
            theirs[r, :n] = first.astype(BF16)
            theirs[r, n:] = second.astype(BF16)


def weight_kernel(sizes, at, arrived, inputs, late, tok_hidden, mine):
    n_chip, piece = sizes
    chip, core = at[1], at[2]
    n = late.shape[0]
    for r in range(n_chip):
        start = (2 * (chip ^ r) + core) * piece
        first, second = block_terms(late[...], tok_hidden[...], inputs, arrived, start, piece)
        mine[r, :n] = first
        mine[r, n:] = second


def add_kernel(n_early, mine, theirs, own, other, *refs):
    n_chip, m, _ = mine.shape
    outs = refs[-n_chip:]
    for r in range(n_chip):
        outs[r][:m] = (mine[r] + theirs[r].astype(F32)).astype(outs[r].dtype)
        if r and n_early:
            for k, lanes in enumerate(early_lanes(own.shape[0])):
                half = own if k < own.shape[0] // TILE else other
                block = k % (own.shape[0] // TILE)
                outs[r][m:, lanes] = half[block * TILE : (block + 1) * TILE]


def early_lanes(rows):
    return [slice(k * LANES, (k + 1) * LANES) for k in range(2 * rows // TILE)]


def row_kernel(n_expert, blocks, at, tok_gate, tok_up, gate, up, behind, out):
    del behind
    size = tok_gate.shape[0] // n_expert
    step = gate.shape[1] // blocks
    for j in range(blocks):
        lanes = slice(j * step, (j + 1) * step)
        total = dot(tok_gate[...], gate[:, lanes], (1, 0)) + dot(tok_up[...], up[:, lanes], (1, 0))
        for r in range(n_expert):
            out[at[0] ^ r, :, lanes] = total[r * size : (r + 1) * size].astype(out.dtype)


def router_kernel(experts, n_expert, at, *refs):
    scores, (packed, normed, router, other, own, through) = refs[:n_expert], refs[n_expert:]
    picked = scores[0][...]
    for s in scores[1:]:
        picked = picked + s[...]
    picked = picked[:, :experts]
    half = normed.shape[1] // 2
    tail = packed[:, half:].astype(F32)
    weight = tail[:, :experts] + tail[:, experts : 2 * experts] + tail[:, 2 * experts : 3 * experts]
    code = tail[:, 3 * experts : 4 * experts]
    grad = jnp.where(code > 0.5, picked - weight * jnp.sum(picked, axis=1, keepdims=True), 0.0)
    high, low = split_high_low(grad)
    core = at[2]
    for out, part in ((other, 1 - core), (own, core)):
        values = normed[:, pl.ds(pl.multiple_of(part * half, LANES), half)]
        out[...] = dot(high, values, (0, 0)) + dot(low, values, (0, 0))
    through[...] = dot(high, router[...], (1, 0)) + dot(low, router[...], (1, 0))


def terms_kernel(count, *refs):
    terms, out = refs[:count], refs[-1]
    while len(terms) > 1:
        terms = [terms[k][...].astype(F32) + terms[k + 1][...].astype(F32) for k in range(0, len(terms), 2)]
    out[...] = terms[0].astype(out.dtype)


def finish_kernel(sizes, at, *refs):
    n_chip, exp_dev, hidden_units, slots_each, n_early = sizes
    pieces, own, other, rows = refs[:n_chip], refs[n_chip], refs[n_chip + 1], refs[n_chip + 2]
    mine, theirs, through, back = refs[n_chip + 3 : n_chip + 7]
    grad_normed, router_grad, *outs = refs[-5:]
    chip, core = at[1], at[2]
    half = mine.shape[1]
    router_grad[:, pl.ds(pl.multiple_of(core * half, LANES), half)] = mine[...]
    router_grad[:, pl.ds(pl.multiple_of((1 - core) * half, LANES), half)] = theirs[...]
    rows_total = through[...]
    for r in range(back.shape[0]):
        rows_total = rows_total + back[r].astype(F32)
    grad_normed[...] = rows_total.astype(grad_normed.dtype)
    m = pieces[0].shape[0]
    n = m - exp_dev * hidden_units
    total = pieces[0][...]
    for piece in pieces[1:]:
        total = total + piece[:m].astype(F32)
    if n_early:
        count = n_early * hidden_units
        held, depth = own.shape[0], rows.shape[1]
        row, column = iota((2 * count, held), 0), iota((2 * count, held), 1)
        spread = (column == (row // count) * hidden_units + row % hidden_units).astype(F32).astype(BF16)
        same = (iota((2 * count, LANES), 0) % count) // hidden_units == iota((2 * count, LANES), 1) // slots_each
        early = jnp.zeros((2 * count, rows.shape[2]), F32)
        for r in range(n_chip):
            for c in range(2):
                if r:
                    half = early_lanes(held)[c * held // TILE : (c + 1) * held // TILE]
                    narrow = jnp.concatenate([pieces[r][m:, lanes] for lanes in half], axis=0)
                else:
                    narrow = (own, other)[c][...]
                wide = jnp.where(same, dot(spread, narrow, (1, 0)), 0.0).astype(BF16)
                early = early + dot(wide[:, :depth], rows[2 * (chip ^ r) + (core ^ c)], (1, 0))
    for k in range(2):
        for e in range(exp_dev):
            if e < n_early:
                first = (k * n_early + e) * hidden_units
                outs[k][:, e, :] = early[first : first + hidden_units]
            else:
                first = (k * (exp_dev - n_early) + e - n_early) * hidden_units
                outs[k][:, e, :] = total[first : first + hidden_units]
    for e in range(exp_dev):
        outs[2][:, e, :] = total[n + e * hidden_units : n + (e + 1) * hidden_units]


def on_device(normed, upstream, expert_ids, router_weight, gate_weight, up_weight, down_weight, saved_inputs):
    n_expert = lax.axis_size("expert")
    n_dp = lax.axis_size("dp")
    n_chip = n_dp // 2
    me = lax.axis_index("expert")
    dp = lax.axis_index("dp")
    core = dp & 1
    chip = dp >> 1
    exp_dev, hidden_units, width = gate_weight.shape
    capacity = saved_inputs.shape[3]
    experts = exp_dev * n_expert
    tokens_here = normed.shape[0]
    tokens = tokens_here * n_expert
    slots = exp_dev * capacity * n_expert
    hidden_all = exp_dev * hidden_units
    piece = width // n_dp
    half = width // 2
    even = piece % LANES == 0
    slots_each = capacity * n_expert
    narrow = -(-2 * hidden_units // TILE) * TILE
    n_early = EARLY * exp_dev // 4
    early_rows = -(-n_early * slots_each // TILE) * TILE
    if not even or early_rows > min(LANES, slots) or 2 * narrow // TILE * LANES > piece:
        n_early = 0
    late_rows = -(-2 * (exp_dev - n_early) * hidden_units // TILE) * TILE
    sent_rows = late_rows + hidden_all
    shape = jax.ShapeDtypeStruct

    def over_expert(value, k):
        return lax.ppermute(value, "expert", [(i, i ^ k) for i in range(n_expert)])

    def over_core(value):
        return lax.ppermute(value, "dp", [(i, i ^ 1) for i in range(n_dp)])

    def over_chip(value, k):
        return lax.ppermute(value, "dp", [(i, i ^ (2 * k)) for i in range(n_dp)])

    def in_hbm(*values):
        return [pltpu.with_memory_space_constraint(value, pltpu.HBM) for value in values]

    def call(kernel, name, outs, args, scalars=False, behind=0):
        specs = [pl.BlockSpec(memory_space=pltpu.VMEM)] * len(args)
        if scalars:
            specs[0] = pl.BlockSpec(memory_space=pltpu.SMEM)
        for k in range(behind):
            specs[-1 - k] = pl.BlockSpec(memory_space=pl.ANY)
        return pl.pallas_call(
            kernel,
            out_shape=outs,
            in_specs=specs,
            out_specs=[pl.BlockSpec(memory_space=pltpu.VMEM)] * len(outs),
            compiler_params=pltpu.CompilerParams(vmem_limit_bytes=VMEM_BYTES),
            cost_estimate=pl.CostEstimate(flops=0, bytes_accessed=0, transcendentals=0),
            name=name,
        )(*args)

    at = jnp.stack([me, chip, core]).astype(jnp.int32)
    router = router_weight.T
    first, packed = pl.pallas_call(
        functools.partial(route_kernel, experts),
        out_shape=[shape((tokens_here, half), BF16), shape((tokens_here, half + LANES), BF16)],
        in_specs=[pl.BlockSpec(memory_space=pltpu.HBM)] * 4,
        out_specs=[pl.BlockSpec(memory_space=pltpu.VMEM)] * 2,
        scratch_shapes=[
            pltpu.VMEM(expert_ids.shape[::-1], jnp.int32),
            pltpu.VMEM((tokens_here, width), BF16),
            pltpu.VMEM((experts, width), BF16),
            pltpu.VMEM((tokens_here, width), BF16),
            pltpu.SemaphoreType.DMA((4,)),
        ],
        compiler_params=pltpu.CompilerParams(vmem_limit_bytes=VMEM_BYTES),
        cost_estimate=pl.CostEstimate(flops=0, bytes_accessed=0, transcendentals=0),
        name="route",
    )(*in_hbm(expert_ids.T, normed, router, upstream))
    if n_expert == 4:
        first_1, second_2 = over_expert(first, 1), over_expert(packed, 2)
        second_1, first_2 = over_expert(packed, 1), over_expert(first, 2)
        firsts = [first, first_1, first_2, over_expert(first_1, 2)]
        seconds = [packed, second_1, second_2, over_expert(second_2, 1)]
    else:
        firsts = [first] + [over_expert(first, k) for k in range(1, n_expert)]
        seconds = [packed] + [over_expert(packed, k) for k in range(1, n_expert)]

    blocks = n_dp if even else 8
    sources = [jnp.transpose(saved_inputs[0], (0, 2, 1, 3)).reshape(exp_dev * capacity, n_expert, width)]
    sources += [jnp.transpose(w, (1, 0, 2)) for w in (gate_weight, up_weight, down_weight)]
    results = (
        [shape((slots, width), BF16)]
        + [shape((hidden_all, width), BF16)] * 3
        + [shape((slots, hidden_all), F32)] * 2
        + [shape((n_dp, early_rows, piece), BF16)] * bool(n_early)
    )
    inputs, gate, up, down, pre_gate, pre_up, *early_x = pl.pallas_call(
        functools.partial(prepare_kernel, n_early, blocks),
        out_shape=results,
        in_specs=[pl.BlockSpec(memory_space=pltpu.HBM)] * 4,
        out_specs=[pl.BlockSpec(memory_space=pltpu.VMEM)] * len(results),
        scratch_shapes=[pltpu.VMEM(source.shape, BF16) for source in sources]
        + [pltpu.SemaphoreType.DMA((4 * blocks,))],
        compiler_params=pltpu.CompilerParams(vmem_limit_bytes=VMEM_BYTES),
        cost_estimate=pl.CostEstimate(flops=0, bytes_accessed=0, transcendentals=0),
        name="prepare",
    )(*in_hbm(*sources))
    if n_early:
        early_x = lax.all_to_all(early_x[0], "dp", 0, 0, tiled=True)

    outs = call(
        functools.partial(expert_kernel, (n_expert, exp_dev, capacity, tokens_here, n_chip, piece, n_early, even)),
        "experts",
        [shape((tokens_here, LANES), F32)] * n_expert
        + [shape((tokens, hidden_all), BF16)] * 2
        + [shape((hidden_all, tokens), BF16), shape((late_rows, slots), BF16), shape((narrow, LANES), BF16)]
        + [shape((tokens, width), BF16)]
        + [shape((n_chip, sent_rows, piece), BF16)] * even,
        (at, *firsts, *seconds, down, pre_gate, pre_up, inputs),
        scalars=True,
    )
    scores = outs[:n_expert]
    tok_gate, tok_up, tok_hidden, slot_late, own_narrow, arrived = outs[n_expert : n_expert + 6]
    back_scores = [scores[0]] + [over_expert(scores[k], k) for k in range(1, n_expert)]
    other_narrow = over_core(own_narrow) if n_early else own_narrow
    if even:
        from_core = over_core(outs[n_expert + 6])
        sent = shape((sent_rows + TILE * bool(n_early), piece), BF16)
        (mine,) = call(
            functools.partial(weight_kernel, (n_chip, piece)),
            "weight_terms",
            [shape((n_chip, sent_rows, piece), F32)],
            (at, arrived, inputs, slot_late, tok_hidden),
            scalars=True,
        )
        chip_sums = call(
            functools.partial(add_kernel, n_early),
            "core_sum",
            [shape((sent_rows, piece), F32)] + [sent] * (n_chip - 1),
            (mine, from_core, own_narrow, other_narrow, *back_scores[1:]),
            behind=n_expert - 1,
        )
    else:
        terms = [dot(slot_late, inputs, (1, 0)), dot(tok_hidden, arrived, (1, 0))]
        terms = jnp.concatenate(terms, axis=0).reshape(sent_rows, n_chip, 2, piece)
        terms = jnp.transpose(terms, (2, 1, 0, 3))
        from_core = over_core(terms[1 - core].astype(BF16))
        terms = terms[core] + from_core.astype(F32)
        chip_sums = [terms[chip ^ k].astype(BF16 if k else F32) for k in range(n_chip)]
    moved = {k: over_chip(chip_sums[k], k) for k in range(n_chip - 1, 0, -1)}
    chip_pieces = [chip_sums[0]] + [moved[k] for k in range(1, n_chip)]

    always = dp < n_dp

    def add_terms(terms, dtype, *behind):
        kernel = functools.partial(terms_kernel, len(terms))
        return call(kernel, "add_terms", [shape(terms[0].shape, dtype)], (*terms, *behind), behind=len(behind))[0]

    def sum_over(total, move, count, dtype, at_once, *behind):
        if at_once:
            return add_terms([total] + [move(total, k) for k in range(1, count)], dtype, *behind)
        rounds = count.bit_length() - 1
        for k in range(rounds):
            last = k == rounds - 1
            total = add_terms([total, move(total, 1 << k)], dtype if last else BF16, *behind * last)
        return total

    def sum_chips(total):
        total = sum_over(total, over_chip, n_chip, F32, False)
        return total, over_core(total)

    def way_back(values):
        back_scores, packed, normed, router, tok_gate, tok_up, gate, up = values
        other, own, through = call(
            functools.partial(router_kernel, experts, n_expert),
            "router_terms",
            [shape((experts, half), F32)] * 2 + [shape((tokens_here, width), F32)],
            (at, *back_scores, packed, normed, router),
            scalars=True,
        )
        (row_pieces,) = call(
            functools.partial(row_kernel, n_expert, 8),
            "row_terms",
            [shape((n_expert, tokens_here, width), BF16)],
            (at, tok_gate, tok_up, gate, up, other),
            scalars=True,
            behind=1,
        )
        total = add_terms([own, over_core(other)], BF16)
        total = sum_over(total, over_expert, n_expert, BF16, False, row_pieces)
        row_pieces, total = lax.optimization_barrier((row_pieces, total))
        back_rows = lax.all_to_all(row_pieces, "expert", 0, 0, tiled=True)
        mine, theirs = lax.cond(always, sum_chips, lambda total: (jnp.zeros((experts, half), F32),) * 2, total)
        return mine, theirs, through, back_rows

    first_score, _ = lax.optimization_barrier((back_scores[0], chip_sums[0]))
    back_scores = [first_score] + back_scores[1:]
    outs = [shape((experts, half), F32)] * 2 + [shape((tokens_here, width), F32)]
    outs += [shape((n_expert, tokens_here, width), BF16)]
    back = lax.cond(
        always,
        way_back,
        lambda values: tuple(jnp.zeros(o.shape, o.dtype) for o in outs),
        (back_scores, packed, normed, router, tok_gate, tok_up, gate, up),
    )
    if not n_early:
        early_x = jnp.zeros((TILE, LANES), BF16)
    grad_normed, router_grad, *grads = call(
        functools.partial(finish_kernel, (n_chip, exp_dev, hidden_units, slots_each, n_early)),
        "finish",
        [shape((tokens_here, width), BF16), shape((experts, width), F32)]
        + [shape((hidden_units, exp_dev, piece), F32)] * 3,
        (at, *chip_pieces, own_narrow, other_narrow, early_x, *back),
        scalars=True,
    )
    grads = [jnp.transpose(g, (1, 0, 2)) for g in grads]
    return (grad_normed, router_grad.T, *grads)


def solution(mesh):
    placed = (
        P(("dp", "expert"), None),
        P(("dp", "expert"), None),
        P(("dp", "expert"), None),
        P(),
        P("expert", None, None),
        P("expert", None, None),
        P("expert", None, None),
        P("dp", "expert", None, None, None),
    )
    return jax.shard_map(
        on_device,
        mesh=mesh,
        in_specs=placed,
        out_specs=(
            P(("dp", "expert"), None),
            P(),
            P("expert", None, "dp"),
            P("expert", None, "dp"),
            P("expert", None, "dp"),
        ),
        check_vma=False,
    )
```

```python
import functools

import jax
import jax.numpy as jnp
from jax import lax
from jax.experimental import pallas as pl
from jax.experimental.pallas import tpu as pltpu
from jax.sharding import PartitionSpec as P

F32 = jnp.float32
BF16 = jnp.bfloat16
LANES = 128
VMEM_BYTES = 16 * 2**20


def dot(left, right, contract):
    return lax.dot_general(
        left,
        right,
        ((contract[:1], contract[1:]), ((), ())),
        preferred_element_type=F32,
    )


def iota(shape, dim):
    return lax.broadcasted_iota(jnp.int32, shape, dim)


def split_high_low(value):
    high = value.astype(BF16)
    return high, (value - high.astype(F32)).astype(BF16)


def route_kernel(experts, *refs):
    sources, (first, packed, ids, normed, router, upstream, sems) = refs[:4], refs[4:]
    tokens, width = normed.shape
    half = width // 2
    copies = [
        pltpu.make_async_copy(source, target, sems.at[k])
        for k, (source, target) in enumerate(zip(sources, (ids, normed, router, upstream)))
    ]
    for copy in copies:
        copy.start()
    copies[0].wait()
    expert = iota((experts, tokens), 0)
    named_t = expert < 0
    for k in range(ids.shape[0]):
        named_t = named_t | (ids[k : k + 1, :] == expert)
    unit = (iota((tokens, tokens), 0) == iota((tokens, tokens), 1)).astype(F32).astype(BF16)
    named_f = dot(unit, named_t.astype(F32).astype(BF16), (1, 1))
    named = named_f > 0.5
    earlier = (iota((tokens, tokens), 1) < iota((tokens, tokens), 0)).astype(F32).astype(BF16)
    slot = dot(earlier, named_f.astype(BF16), (1, 0))
    code = jnp.where(named, slot + 1.0, 0.0)
    copies[1].wait()
    copies[2].wait()
    logits = dot(normed[...], router[...], (1, 1))
    largest = jnp.max(jnp.where(named, logits, -jnp.inf), axis=1, keepdims=True)
    weight = jnp.where(named, jnp.exp(jnp.where(named, logits - largest, 0.0)), 0.0)
    weight = weight / jnp.sum(weight, axis=1, keepdims=True)
    high = weight.astype(BF16).astype(F32)
    middle = (weight - high).astype(BF16).astype(F32)
    low = weight - high - middle
    rest = jnp.zeros((tokens, LANES - 4 * experts), F32)
    packed[:, half:] = jnp.concatenate([high, middle, low, code, rest], axis=1).astype(BF16)
    copies[3].wait()
    first[...] = upstream[:, :half]
    packed[:, :half] = upstream[:, half:]


def prepare_kernel(blocks, *refs):
    sources, refs = refs[:4], refs[4:]
    scratch, sems, refs = refs[-5:-1], refs[-1], refs[:-5]
    inputs, gate_rows, up_rows, down_rows, pre_gate, pre_up = refs
    step = inputs.shape[1] // blocks
    copies = []
    for j in range(blocks):
        lanes = pl.ds(j * step, step)
        for k in range(4):
            copy = pltpu.make_async_copy(sources[k].at[:, :, lanes], scratch[k].at[:, :, lanes], sems.at[4 * j + k])
            copy.start()
            copies.append(copy)
    pre_gate[...] = jnp.zeros_like(pre_gate)
    pre_up[...] = jnp.zeros_like(pre_up)
    for j in range(blocks):
        lanes = slice(j * step, (j + 1) * step)
        for k, target in enumerate((inputs, gate_rows, up_rows, down_rows)):
            copies[4 * j + k].wait()
            target[:, lanes] = scratch[k][:, :, lanes].reshape(target.shape[0], step)
        pre_gate[...] += dot(inputs[:, lanes], gate_rows[:, lanes], (1, 1))
        pre_up[...] += dot(inputs[:, lanes], up_rows[:, lanes], (1, 1))


def pick(expert_of_column, experts, groups, columns):
    lane = iota((LANES, columns), 0)
    out = lane < 0
    for g in groups:
        out = out | (lane == expert_of_column + g * experts)
    return out.astype(F32).astype(BF16)


def block_terms(turned, inputs, arrived, start, piece):
    gate, up, hidden = turned
    at = pl.ds(pl.multiple_of(start, LANES), piece)
    return [dot(gate, inputs[:, at], (1, 0)), dot(up, inputs[:, at], (1, 0)), dot(hidden, arrived[:, at], (1, 0))]


def expert_kernel(sizes, at, *refs):
    n_expert, exp_dev, capacity, tokens_here = sizes
    firsts, seconds, rest = refs[:n_expert], refs[n_expert : 2 * n_expert], refs[2 * n_expert :]
    down, pre_gate, pre_up = rest[:3]
    scores = rest[3 : 3 + n_expert]
    place, slot_gate, slot_up, slot_hidden, arrived = rest[3 + n_expert :]
    me = at[0]
    experts = exp_dev * n_expert
    tokens = tokens_here * n_expert
    hidden_all, width = down.shape
    half = width // 2
    slots = exp_dev * capacity * n_expert
    packed = jnp.concatenate([u[:, half:] for u in seconds], axis=0)
    for r in range(n_expert):
        rows = slice(r * tokens_here, (r + 1) * tokens_here)
        arrived[rows, :half] = firsts[r][...]
        arrived[rows, half:] = seconds[r][:, :half]
    grad_hidden_raw = dot(arrived[...], down[...], (1, 1))

    expert_of_hidden = me * exp_dev + iota((LANES, hidden_all), 1) % exp_dev
    weight_hidden = dot(packed, pick(expert_of_hidden, experts, (0, 1, 2), hidden_all), (1, 0))
    expert_of_slot = me * exp_dev + iota((LANES, slots), 1) // (capacity * n_expert)
    code_at = dot(packed, pick(expert_of_slot, experts, (3,), slots), (1, 0))
    column = iota((tokens, slots), 1)
    source = me ^ (iota((tokens, slots), 0) // tokens_here)
    slot_code = ((column // n_expert) % capacity + 1).astype(F32)
    chosen = (source == column % n_expert) & (jnp.abs(code_at - slot_code) < 0.5)
    placed = chosen.astype(F32).astype(BF16)
    place[...] = placed

    high, low = split_high_low(grad_hidden_raw * weight_hidden)
    grad_hidden = dot(placed, high, (0, 0)) + dot(placed, low, (0, 0))
    same = iota((slots, hidden_all), 1) % exp_dev == iota((slots, hidden_all), 0) // (capacity * n_expert)
    v = pre_gate[...]
    logistic = jax.nn.sigmoid(v)
    activated = v * logistic
    hidden = jnp.where(same, activated * pre_up[...], 0.0).astype(BF16)
    slope = logistic * (1.0 + v * (1.0 - logistic))
    slot_hidden[...] = hidden
    slot_gate[...] = jnp.where(same, grad_hidden * pre_up[...] * slope, 0.0).astype(BF16)
    slot_up[...] = jnp.where(same, grad_hidden * activated, 0.0).astype(BF16)
    score = jnp.sum(hidden.astype(F32) * grad_hidden, axis=1, keepdims=True)
    expert_of_row = me * exp_dev + iota((slots, LANES), 0) // (capacity * n_expert)
    score = jnp.where(iota((slots, LANES), 1) == expert_of_row, score, 0.0)
    high, low = split_high_low(score)
    picked = dot(placed, high, (1, 0)) + dot(placed, low, (1, 0))
    for r in range(n_expert):
        scores[r][...] = picked[r * tokens_here : (r + 1) * tokens_here]


def core_kernel(sizes, at, *refs):
    n_expert, exp_dev, n_chip, piece, even = sizes
    seconds, rest = refs[:n_expert], refs[n_expert:]
    place, slot_gate, slot_up, slot_hidden, arrived, inputs = rest[:6]
    tok_gate, tok_up, turned_gate, turned_up, turned_hidden = rest[6:11]
    me, chip, core = at[0], at[1], at[2]
    experts = exp_dev * n_expert
    hidden_all = slot_gate.shape[1]
    hidden_units = hidden_all // exp_dev
    half = arrived.shape[1] // 2
    packed = jnp.concatenate([u[:, half:] for u in seconds], axis=0)
    expert_of_hidden = me * exp_dev + iota((LANES, hidden_all), 1) % exp_dev
    weight_hidden = dot(packed, pick(expert_of_hidden, experts, (0, 1, 2), hidden_all), (1, 0))
    scaled_hidden = (dot(place[...], slot_hidden[...], (1, 0)) * weight_hidden).astype(BF16)
    row, column = iota((hidden_all, hidden_all), 0), iota((hidden_all, hidden_all), 1)
    order = row == (column % exp_dev) * hidden_units + column // exp_dev
    order = order.astype(F32).astype(BF16)
    turned = [dot(order, value, (1, 1)).astype(BF16) for value in (slot_gate[...], slot_up[...], scaled_hidden)]
    turned_gate[...], turned_up[...], turned_hidden[...] = turned
    if even:
        theirs = rest[11]
        for r in range(n_chip):
            terms = block_terms(turned, inputs, arrived, (2 * (chip ^ r) + 1 - core) * piece, piece)
            for k in range(3):
                theirs[r, k * hidden_all : (k + 1) * hidden_all] = terms[k].astype(BF16)
    tok_gate[...] = dot(place[...], slot_gate[...], (1, 0)).astype(BF16)
    tok_up[...] = dot(place[...], slot_up[...], (1, 0)).astype(BF16)


def weight_kernel(sizes, at, arrived, inputs, gate, up, hidden, mine):
    n_chip, piece = sizes
    chip, core = at[1], at[2]
    n = gate.shape[0]
    for r in range(n_chip):
        start = (2 * (chip ^ r) + core) * piece
        terms = block_terms((gate[...], up[...], hidden[...]), inputs, arrived, start, piece)
        for k in range(3):
            mine[r, k * n : (k + 1) * n] = terms[k]


def add_kernel(mine, theirs, *outs):
    for r in range(len(outs)):
        outs[r][...] = (mine[r] + theirs[r].astype(F32)).astype(outs[r].dtype)


def row_kernel(n_expert, blocks, at, tok_gate, tok_up, gate, up, behind, out):
    del behind
    size = tok_gate.shape[0] // n_expert
    step = gate.shape[1] // blocks
    for j in range(blocks):
        lanes = slice(j * step, (j + 1) * step)
        total = dot(tok_gate[...], gate[:, lanes], (1, 0)) + dot(tok_up[...], up[:, lanes], (1, 0))
        for r in range(n_expert):
            out[at[0] ^ r, :, lanes] = total[r * size : (r + 1) * size].astype(out.dtype)


def router_kernel(experts, n_expert, at, *refs):
    scores, (packed, normed, router, other, own, through) = refs[:n_expert], refs[n_expert:]
    picked = scores[0][...]
    for s in scores[1:]:
        picked = picked + s[...]
    picked = picked[:, :experts]
    half = normed.shape[1] // 2
    tail = packed[:, half:].astype(F32)
    weight = tail[:, :experts] + tail[:, experts : 2 * experts] + tail[:, 2 * experts : 3 * experts]
    code = tail[:, 3 * experts : 4 * experts]
    grad = jnp.where(code > 0.5, picked - weight * jnp.sum(picked, axis=1, keepdims=True), 0.0)
    high, low = split_high_low(grad)
    core = at[2]
    for out, part in ((other, 1 - core), (own, core)):
        values = normed[:, pl.ds(pl.multiple_of(part * half, LANES), half)]
        out[...] = dot(high, values, (0, 0)) + dot(low, values, (0, 0))
    through[...] = dot(high, router[...], (1, 0)) + dot(low, router[...], (1, 0))


def terms_kernel(count, *refs):
    terms, out = refs[:count], refs[-1]
    while len(terms) > 1:
        terms = [terms[k][...].astype(F32) + terms[k + 1][...].astype(F32) for k in range(0, len(terms), 2)]
    out[...] = terms[0].astype(out.dtype)


def finish_kernel(sizes, at, *refs):
    exp_dev, hidden_units = sizes
    pieces, (mine, theirs, through, back) = refs[:-9], refs[-9:-5]
    grad_normed, router_grad, *outs = refs[-5:]
    core = at[2]
    half = mine.shape[1]
    router_grad[:, pl.ds(pl.multiple_of(core * half, LANES), half)] = mine[...]
    router_grad[:, pl.ds(pl.multiple_of((1 - core) * half, LANES), half)] = theirs[...]
    rows_total = through[...]
    for r in range(back.shape[0]):
        rows_total = rows_total + back[r].astype(F32)
    grad_normed[...] = rows_total.astype(grad_normed.dtype)
    total = pieces[0][...]
    for piece in pieces[1:]:
        total = total + piece[...].astype(F32)
    for k in range(3):
        for e in range(exp_dev):
            first = (k * exp_dev + e) * hidden_units
            outs[k][:, e, :] = total[first : first + hidden_units]


def on_device(normed, upstream, expert_ids, router_weight, gate_weight, up_weight, down_weight, saved_inputs):
    n_expert = lax.axis_size("expert")
    n_dp = lax.axis_size("dp")
    n_chip = n_dp // 2
    me = lax.axis_index("expert")
    dp = lax.axis_index("dp")
    core = dp & 1
    chip = dp >> 1
    exp_dev, hidden_units, width = gate_weight.shape
    capacity = saved_inputs.shape[3]
    experts = exp_dev * n_expert
    tokens_here = normed.shape[0]
    tokens = tokens_here * n_expert
    slots = exp_dev * capacity * n_expert
    hidden_all = exp_dev * hidden_units
    piece = width // n_dp
    half = width // 2
    even = piece % LANES == 0
    shape = jax.ShapeDtypeStruct

    def over_expert(value, k):
        return lax.ppermute(value, "expert", [(i, i ^ k) for i in range(n_expert)])

    def over_core(value):
        return lax.ppermute(value, "dp", [(i, i ^ 1) for i in range(n_dp)])

    def over_chip(value, k):
        return lax.ppermute(value, "dp", [(i, i ^ (2 * k)) for i in range(n_dp)])

    def in_hbm(*values):
        return [pltpu.with_memory_space_constraint(value, pltpu.HBM) for value in values]

    def call(kernel, name, outs, args, scalars=False, behind=0):
        specs = [pl.BlockSpec(memory_space=pltpu.VMEM)] * len(args)
        if scalars:
            specs[0] = pl.BlockSpec(memory_space=pltpu.SMEM)
        for k in range(behind):
            specs[-1 - k] = pl.BlockSpec(memory_space=pl.ANY)
        return pl.pallas_call(
            kernel,
            out_shape=outs,
            in_specs=specs,
            out_specs=[pl.BlockSpec(memory_space=pltpu.VMEM)] * len(outs),
            compiler_params=pltpu.CompilerParams(vmem_limit_bytes=VMEM_BYTES),
            cost_estimate=pl.CostEstimate(flops=0, bytes_accessed=0, transcendentals=0),
            name=name,
        )(*args)

    at = jnp.stack([me, chip, core]).astype(jnp.int32)
    router = router_weight.T
    first, packed = pl.pallas_call(
        functools.partial(route_kernel, experts),
        out_shape=[shape((tokens_here, half), BF16), shape((tokens_here, half + LANES), BF16)],
        in_specs=[pl.BlockSpec(memory_space=pltpu.HBM)] * 4,
        out_specs=[pl.BlockSpec(memory_space=pltpu.VMEM)] * 2,
        scratch_shapes=[
            pltpu.VMEM(expert_ids.shape[::-1], jnp.int32),
            pltpu.VMEM((tokens_here, width), BF16),
            pltpu.VMEM((experts, width), BF16),
            pltpu.VMEM((tokens_here, width), BF16),
            pltpu.SemaphoreType.DMA((4,)),
        ],
        compiler_params=pltpu.CompilerParams(vmem_limit_bytes=VMEM_BYTES),
        cost_estimate=pl.CostEstimate(flops=0, bytes_accessed=0, transcendentals=0),
        name="route",
    )(*in_hbm(expert_ids.T, normed, router, upstream))
    if n_expert == 4:
        first_1, second_2 = over_expert(first, 1), over_expert(packed, 2)
        second_1, first_2 = over_expert(packed, 1), over_expert(first, 2)
        firsts = [first, first_1, first_2, over_expert(first_1, 2)]
        seconds = [packed, second_1, second_2, over_expert(second_2, 1)]
    else:
        firsts = [first] + [over_expert(first, k) for k in range(1, n_expert)]
        seconds = [packed] + [over_expert(packed, k) for k in range(1, n_expert)]

    blocks = n_dp if even else 8
    sources = [jnp.transpose(saved_inputs[0], (0, 2, 1, 3)).reshape(exp_dev * capacity, n_expert, width)]
    sources += [jnp.transpose(w, (1, 0, 2)) for w in (gate_weight, up_weight, down_weight)]
    results = (
        [shape((slots, width), BF16)]
        + [shape((hidden_all, width), BF16)] * 3
        + [shape((slots, hidden_all), F32)] * 2
    )
    inputs, gate, up, down, pre_gate, pre_up = pl.pallas_call(
        functools.partial(prepare_kernel, blocks),
        out_shape=results,
        in_specs=[pl.BlockSpec(memory_space=pltpu.HBM)] * 4,
        out_specs=[pl.BlockSpec(memory_space=pltpu.VMEM)] * len(results),
        scratch_shapes=[pltpu.VMEM(source.shape, BF16) for source in sources]
        + [pltpu.SemaphoreType.DMA((4 * blocks,))],
        compiler_params=pltpu.CompilerParams(vmem_limit_bytes=VMEM_BYTES),
        cost_estimate=pl.CostEstimate(flops=0, bytes_accessed=0, transcendentals=0),
        name="prepare",
    )(*in_hbm(*sources))

    outs = call(
        functools.partial(expert_kernel, (n_expert, exp_dev, capacity, tokens_here)),
        "experts",
        [shape((tokens_here, LANES), F32)] * n_expert
        + [shape((tokens, slots), BF16)]
        + [shape((slots, hidden_all), BF16)] * 3
        + [shape((tokens, width), BF16)],
        (at, *firsts, *seconds, down, pre_gate, pre_up),
        scalars=True,
    )
    scores, by_slot, arrived = outs[:n_expert], outs[n_expert:-1], outs[-1]
    back_scores = [scores[0]] + [over_expert(scores[k], k) for k in range(1, n_expert)]
    tok_gate, tok_up, *turned = call(
        functools.partial(core_kernel, (n_expert, exp_dev, n_chip, piece, even)),
        "core_terms",
        [shape((tokens, hidden_all), BF16)] * 2
        + [shape((hidden_all, slots), BF16)] * 2
        + [shape((hidden_all, tokens), BF16)]
        + [shape((n_chip, 3 * hidden_all, piece), BF16)] * even,
        (at, *seconds, *by_slot, arrived, inputs),
        scalars=True,
    )
    turned, theirs = turned[:3], turned[3:]
    if even:
        from_core = over_core(theirs[0])
        (mine,) = call(
            functools.partial(weight_kernel, (n_chip, piece)),
            "weight_terms",
            [shape((n_chip, 3 * hidden_all, piece), F32)],
            (at, arrived, inputs, *turned),
            scalars=True,
        )
    if even:
        chip_sums = call(
            add_kernel,
            "core_sum",
            [shape((3 * hidden_all, piece), BF16 if k else F32) for k in range(n_chip)],
            (mine, from_core),
        )
    else:
        terms = [dot(turned[0], inputs, (1, 0)), dot(turned[1], inputs, (1, 0)), dot(turned[2], arrived, (1, 0))]
        terms = jnp.concatenate(terms, axis=0).reshape(3 * hidden_all, n_chip, 2, piece)
        terms = jnp.transpose(terms, (2, 1, 0, 3))
        from_core = over_core(terms[1 - core].astype(BF16))
        terms = terms[core] + from_core.astype(F32)
        chip_sums = [terms[chip ^ k].astype(BF16 if k else F32) for k in range(n_chip)]
    chip_sums, back_scores = lax.optimization_barrier((chip_sums, back_scores))
    moved = {k: over_chip(chip_sums[k], k) for k in range(n_chip - 1, 1, -1)}

    always = dp < n_dp

    def add_terms(terms, dtype, *behind):
        kernel = functools.partial(terms_kernel, len(terms))
        return call(kernel, "add_terms", [shape(terms[0].shape, dtype)], (*terms, *behind), behind=len(behind))[0]

    def add_pair(total, move, k, dtype=BF16):
        return add_terms([total, move(total, 1 << k)], dtype)

    expert_rounds, chip_rounds = n_expert.bit_length() - 1, n_chip.bit_length() - 1

    def sum_chips(values):
        total, near = values
        for k in range(chip_rounds):
            total = add_pair(total, over_chip, k, F32 if k == chip_rounds - 1 else BF16)
            if k == 0:
                near, total = lax.optimization_barrier((near, total))
                near = over_chip(near, 1)
        return near, total, over_core(total)

    def as_one(function, values):
        outs = jax.eval_shape(function, values)
        return lax.cond(always, function, lambda values: jax.tree.map(lambda o: jnp.zeros(o.shape, o.dtype), outs), values)

    def way_back(values):
        back_scores, packed, normed, router, tok_gate, tok_up, gate, up, near = values
        other, own, through = call(
            functools.partial(router_kernel, experts, n_expert),
            "router_terms",
            [shape((experts, half), F32)] * 2 + [shape((tokens_here, width), F32)],
            (at, *back_scores, packed, normed, router),
            scalars=True,
        )
        (row_pieces,) = call(
            functools.partial(row_kernel, n_expert, 8),
            "row_terms",
            [shape((n_expert, tokens_here, width), BF16)],
            (at, tok_gate, tok_up, gate, up, other),
            scalars=True,
            behind=1,
        )
        total = add_terms([own, over_core(other)], BF16)
        if n_expert == 4:
            total = add_terms([total] + [over_expert(total, k) for k in range(1, n_expert)], BF16)
        else:
            for k in range(expert_rounds):
                total = add_pair(total, over_expert, k)
        row_pieces, total = lax.optimization_barrier((row_pieces, total))
        back_rows = lax.all_to_all(row_pieces, "expert", 0, 0, tiled=True)
        return *as_one(sum_chips, (total, near)), through, back_rows

    near, *back = as_one(way_back, (back_scores, packed, normed, router, tok_gate, tok_up, gate, up, chip_sums[1]))
    chip_pieces = [chip_sums[0], near] + [moved[k] for k in range(2, n_chip)]
    grad_normed, router_grad, *grads = call(
        functools.partial(finish_kernel, (exp_dev, hidden_units)),
        "finish",
        [shape((tokens_here, width), BF16), shape((experts, width), F32)]
        + [shape((hidden_units, exp_dev, piece), F32)] * 3,
        (at, *chip_pieces, *back),
        scalars=True,
    )
    grads = [jnp.transpose(g, (1, 0, 2)) for g in grads]
    return (grad_normed, router_grad.T, *grads)


def solution(mesh):
    placed = (
        P(("dp", "expert"), None),
        P(("dp", "expert"), None),
        P(("dp", "expert"), None),
        P(),
        P("expert", None, None),
        P("expert", None, None),
        P("expert", None, None),
        P("dp", "expert", None, None, None),
    )
    return jax.shard_map(
        on_device,
        mesh=mesh,
        in_specs=placed,
        out_specs=(
            P(("dp", "expert"), None),
            P(),
            P("expert", None, "dp"),
            P("expert", None, "dp"),
            P("expert", None, "dp"),
        ),
        check_vma=False,
    )
```

```python
import functools

import jax
import jax.numpy as jnp
from jax import lax
from jax.experimental import pallas as pl
from jax.experimental.pallas import tpu as pltpu
from jax.sharding import PartitionSpec as P

F32 = jnp.float32
BF16 = jnp.bfloat16
LANES = 128
VMEM_BYTES = 16 * 2**20


def dot(left, right, contract):
    return lax.dot_general(
        left,
        right,
        ((contract[:1], contract[1:]), ((), ())),
        preferred_element_type=F32,
    )


def iota(shape, dim):
    return lax.broadcasted_iota(jnp.int32, shape, dim)


def split_high_low(value):
    high = value.astype(BF16)
    return high, (value - high.astype(F32)).astype(BF16)


def route_kernel(experts, *refs):
    sources, (first, packed, ids, normed, router, upstream, sems) = refs[:4], refs[4:]
    tokens, width = normed.shape
    half = width // 2
    copies = [
        pltpu.make_async_copy(source, target, sems.at[k])
        for k, (source, target) in enumerate(zip(sources, (ids, normed, router, upstream)))
    ]
    for copy in copies:
        copy.start()
    copies[0].wait()
    expert = iota((experts, tokens), 0)
    named_t = expert < 0
    for k in range(ids.shape[0]):
        named_t = named_t | (ids[k : k + 1, :] == expert)
    unit = (iota((tokens, tokens), 0) == iota((tokens, tokens), 1)).astype(F32).astype(BF16)
    named_f = dot(unit, named_t.astype(F32).astype(BF16), (1, 1))
    named = named_f > 0.5
    earlier = (iota((tokens, tokens), 1) < iota((tokens, tokens), 0)).astype(F32).astype(BF16)
    slot = dot(earlier, named_f.astype(BF16), (1, 0))
    code = jnp.where(named, slot + 1.0, 0.0)
    copies[1].wait()
    copies[2].wait()
    logits = dot(normed[...], router[...], (1, 1))
    largest = jnp.max(jnp.where(named, logits, -jnp.inf), axis=1, keepdims=True)
    weight = jnp.where(named, jnp.exp(jnp.where(named, logits - largest, 0.0)), 0.0)
    weight = weight / jnp.sum(weight, axis=1, keepdims=True)
    high = weight.astype(BF16).astype(F32)
    middle = (weight - high).astype(BF16).astype(F32)
    low = weight - high - middle
    rest = jnp.zeros((tokens, LANES - 4 * experts), F32)
    packed[:, half:] = jnp.concatenate([high, middle, low, code, rest], axis=1).astype(BF16)
    copies[3].wait()
    first[...] = upstream[:, :half]
    packed[:, :half] = upstream[:, half:]


def prepare_kernel(blocks, *refs):
    sources, refs = refs[:4], refs[4:]
    scratch, sems, refs = refs[-5:-1], refs[-1], refs[:-5]
    inputs, gate_rows, up_rows, down_rows, pre_gate, pre_up = refs
    step = inputs.shape[1] // blocks
    copies = []
    for j in range(blocks):
        lanes = pl.ds(j * step, step)
        for k in range(4):
            copy = pltpu.make_async_copy(sources[k].at[:, :, lanes], scratch[k].at[:, :, lanes], sems.at[4 * j + k])
            copy.start()
            copies.append(copy)
    pre_gate[...] = jnp.zeros_like(pre_gate)
    pre_up[...] = jnp.zeros_like(pre_up)
    for j in range(blocks):
        lanes = slice(j * step, (j + 1) * step)
        for k, target in enumerate((inputs, gate_rows, up_rows, down_rows)):
            copies[4 * j + k].wait()
            target[:, lanes] = scratch[k][:, :, lanes].reshape(target.shape[0], step)
        pre_gate[...] += dot(inputs[:, lanes], gate_rows[:, lanes], (1, 1))
        pre_up[...] += dot(inputs[:, lanes], up_rows[:, lanes], (1, 1))


def pick(expert_of_column, experts, groups, columns):
    lane = iota((LANES, columns), 0)
    out = lane < 0
    for g in groups:
        out = out | (lane == expert_of_column + g * experts)
    return out.astype(F32).astype(BF16)


def block_terms(turned, inputs, arrived, start, piece):
    gate, up, hidden = turned
    at = pl.ds(pl.multiple_of(start, LANES), piece)
    return [dot(gate, inputs[:, at], (1, 0)), dot(up, inputs[:, at], (1, 0)), dot(hidden, arrived[:, at], (1, 0))]


def expert_kernel(sizes, at, *refs):
    n_expert, exp_dev, capacity, tokens_here = sizes
    firsts, seconds, rest = refs[:n_expert], refs[n_expert : 2 * n_expert], refs[2 * n_expert :]
    down, pre_gate, pre_up = rest[:3]
    scores = rest[3 : 3 + n_expert]
    place, slot_gate, slot_up, slot_hidden, arrived = rest[3 + n_expert :]
    me = at[0]
    experts = exp_dev * n_expert
    tokens = tokens_here * n_expert
    hidden_all, width = down.shape
    half = width // 2
    slots = exp_dev * capacity * n_expert
    packed = jnp.concatenate([u[:, half:] for u in seconds], axis=0)
    for r in range(n_expert):
        rows = slice(r * tokens_here, (r + 1) * tokens_here)
        arrived[rows, :half] = firsts[r][...]
        arrived[rows, half:] = seconds[r][:, :half]
    grad_hidden_raw = dot(arrived[...], down[...], (1, 1))

    expert_of_hidden = me * exp_dev + iota((LANES, hidden_all), 1) % exp_dev
    weight_hidden = dot(packed, pick(expert_of_hidden, experts, (0, 1, 2), hidden_all), (1, 0))
    expert_of_slot = me * exp_dev + iota((LANES, slots), 1) // (capacity * n_expert)
    code_at = dot(packed, pick(expert_of_slot, experts, (3,), slots), (1, 0))
    column = iota((tokens, slots), 1)
    source = me ^ (iota((tokens, slots), 0) // tokens_here)
    slot_code = ((column // n_expert) % capacity + 1).astype(F32)
    chosen = (source == column % n_expert) & (jnp.abs(code_at - slot_code) < 0.5)
    placed = chosen.astype(F32).astype(BF16)
    place[...] = placed

    high, low = split_high_low(grad_hidden_raw * weight_hidden)
    grad_hidden = dot(placed, high, (0, 0)) + dot(placed, low, (0, 0))
    same = iota((slots, hidden_all), 1) % exp_dev == iota((slots, hidden_all), 0) // (capacity * n_expert)
    v = pre_gate[...]
    logistic = jax.nn.sigmoid(v)
    activated = v * logistic
    hidden = jnp.where(same, activated * pre_up[...], 0.0).astype(BF16)
    slope = logistic * (1.0 + v * (1.0 - logistic))
    slot_hidden[...] = hidden
    slot_gate[...] = jnp.where(same, grad_hidden * pre_up[...] * slope, 0.0).astype(BF16)
    slot_up[...] = jnp.where(same, grad_hidden * activated, 0.0).astype(BF16)
    score = jnp.sum(hidden.astype(F32) * grad_hidden, axis=1, keepdims=True)
    expert_of_row = me * exp_dev + iota((slots, LANES), 0) // (capacity * n_expert)
    score = jnp.where(iota((slots, LANES), 1) == expert_of_row, score, 0.0)
    high, low = split_high_low(score)
    picked = dot(placed, high, (1, 0)) + dot(placed, low, (1, 0))
    for r in range(n_expert):
        scores[r][...] = picked[r * tokens_here : (r + 1) * tokens_here]


def core_kernel(sizes, at, *refs):
    n_expert, exp_dev, n_chip, piece, even = sizes
    seconds, rest = refs[:n_expert], refs[n_expert:]
    place, slot_gate, slot_up, slot_hidden, arrived, inputs = rest[:6]
    tok_gate, tok_up, turned_gate, turned_up, turned_hidden = rest[6:11]
    me, chip, core = at[0], at[1], at[2]
    experts = exp_dev * n_expert
    hidden_all = slot_gate.shape[1]
    hidden_units = hidden_all // exp_dev
    half = arrived.shape[1] // 2
    packed = jnp.concatenate([u[:, half:] for u in seconds], axis=0)
    expert_of_hidden = me * exp_dev + iota((LANES, hidden_all), 1) % exp_dev
    weight_hidden = dot(packed, pick(expert_of_hidden, experts, (0, 1, 2), hidden_all), (1, 0))
    scaled_hidden = (dot(place[...], slot_hidden[...], (1, 0)) * weight_hidden).astype(BF16)
    row, column = iota((hidden_all, hidden_all), 0), iota((hidden_all, hidden_all), 1)
    order = row == (column % exp_dev) * hidden_units + column // exp_dev
    order = order.astype(F32).astype(BF16)
    turned = [dot(order, value, (1, 1)).astype(BF16) for value in (slot_gate[...], slot_up[...], scaled_hidden)]
    turned_gate[...], turned_up[...], turned_hidden[...] = turned
    if even:
        theirs = rest[11]
        for r in range(n_chip):
            terms = block_terms(turned, inputs, arrived, (2 * (chip ^ r) + 1 - core) * piece, piece)
            for k in range(3):
                theirs[r, k * hidden_all : (k + 1) * hidden_all] = terms[k].astype(BF16)
    tok_gate[...] = dot(place[...], slot_gate[...], (1, 0)).astype(BF16)
    tok_up[...] = dot(place[...], slot_up[...], (1, 0)).astype(BF16)


def weight_kernel(sizes, at, arrived, inputs, gate, up, hidden, mine):
    n_chip, piece = sizes
    chip, core = at[1], at[2]
    n = gate.shape[0]
    for r in range(n_chip):
        start = (2 * (chip ^ r) + core) * piece
        terms = block_terms((gate[...], up[...], hidden[...]), inputs, arrived, start, piece)
        for k in range(3):
            mine[r, k * n : (k + 1) * n] = terms[k]


def add_kernel(mine, theirs, *outs):
    for r in range(len(outs)):
        outs[r][...] = (mine[r] + theirs[r].astype(F32)).astype(outs[r].dtype)


def row_kernel(n_expert, blocks, at, tok_gate, tok_up, gate, up, behind, out):
    del behind
    size = tok_gate.shape[0] // n_expert
    step = gate.shape[1] // blocks
    for j in range(blocks):
        lanes = slice(j * step, (j + 1) * step)
        total = dot(tok_gate[...], gate[:, lanes], (1, 0)) + dot(tok_up[...], up[:, lanes], (1, 0))
        for r in range(n_expert):
            out[at[0] ^ r, :, lanes] = total[r * size : (r + 1) * size].astype(out.dtype)


def router_kernel(experts, n_expert, at, *refs):
    scores, (packed, normed, router, other, own, through) = refs[:n_expert], refs[n_expert:]
    picked = scores[0][...]
    for s in scores[1:]:
        picked = picked + s[...]
    picked = picked[:, :experts]
    half = normed.shape[1] // 2
    tail = packed[:, half:].astype(F32)
    weight = tail[:, :experts] + tail[:, experts : 2 * experts] + tail[:, 2 * experts : 3 * experts]
    code = tail[:, 3 * experts : 4 * experts]
    grad = jnp.where(code > 0.5, picked - weight * jnp.sum(picked, axis=1, keepdims=True), 0.0)
    high, low = split_high_low(grad)
    core = at[2]
    for out, part in ((other, 1 - core), (own, core)):
        values = normed[:, pl.ds(pl.multiple_of(part * half, LANES), half)]
        out[...] = dot(high, values, (0, 0)) + dot(low, values, (0, 0))
    through[...] = dot(high, router[...], (1, 0)) + dot(low, router[...], (1, 0))


def terms_kernel(count, *refs):
    terms, out = refs[:count], refs[-1]
    while len(terms) > 1:
        terms = [terms[k][...].astype(F32) + terms[k + 1][...].astype(F32) for k in range(0, len(terms), 2)]
    out[...] = terms[0].astype(out.dtype)


def finish_kernel(sizes, at, *refs):
    exp_dev, hidden_units = sizes
    pieces, halves, (through, back) = refs[:-11], refs[-11:-7], refs[-7:-5]
    grad_normed, router_grad, *outs = refs[-5:]
    core = at[2]
    half = halves[0].shape[1]
    for k in range(2):
        lanes = pl.ds(pl.multiple_of((core ^ k) * half, LANES), half)
        router_grad[:, lanes] = halves[2 * k][...].astype(F32) + halves[2 * k + 1][...].astype(F32)
    rows_total = through[...]
    for r in range(back.shape[0]):
        rows_total = rows_total + back[r].astype(F32)
    grad_normed[...] = rows_total.astype(grad_normed.dtype)
    total = pieces[0][...]
    for piece in pieces[1:]:
        total = total + piece[...].astype(F32)
    for k in range(3):
        for e in range(exp_dev):
            first = (k * exp_dev + e) * hidden_units
            outs[k][:, e, :] = total[first : first + hidden_units]


def on_device(normed, upstream, expert_ids, router_weight, gate_weight, up_weight, down_weight, saved_inputs):
    n_expert = lax.axis_size("expert")
    n_dp = lax.axis_size("dp")
    n_chip = n_dp // 2
    me = lax.axis_index("expert")
    dp = lax.axis_index("dp")
    core = dp & 1
    chip = dp >> 1
    exp_dev, hidden_units, width = gate_weight.shape
    capacity = saved_inputs.shape[3]
    experts = exp_dev * n_expert
    tokens_here = normed.shape[0]
    tokens = tokens_here * n_expert
    slots = exp_dev * capacity * n_expert
    hidden_all = exp_dev * hidden_units
    piece = width // n_dp
    half = width // 2
    even = piece % LANES == 0
    shape = jax.ShapeDtypeStruct

    def over_expert(value, k):
        return lax.ppermute(value, "expert", [(i, i ^ k) for i in range(n_expert)])

    def over_core(value):
        return lax.ppermute(value, "dp", [(i, i ^ 1) for i in range(n_dp)])

    def over_chip(value, k):
        return lax.ppermute(value, "dp", [(i, i ^ (2 * k)) for i in range(n_dp)])

    def in_hbm(*values):
        return [pltpu.with_memory_space_constraint(value, pltpu.HBM) for value in values]

    def call(kernel, name, outs, args, scalars=False, behind=0):
        specs = [pl.BlockSpec(memory_space=pltpu.VMEM)] * len(args)
        if scalars:
            specs[0] = pl.BlockSpec(memory_space=pltpu.SMEM)
        for k in range(behind):
            specs[-1 - k] = pl.BlockSpec(memory_space=pl.ANY)
        return pl.pallas_call(
            kernel,
            out_shape=outs,
            in_specs=specs,
            out_specs=[pl.BlockSpec(memory_space=pltpu.VMEM)] * len(outs),
            compiler_params=pltpu.CompilerParams(vmem_limit_bytes=VMEM_BYTES),
            cost_estimate=pl.CostEstimate(flops=0, bytes_accessed=0, transcendentals=0),
            name=name,
        )(*args)

    at = jnp.stack([me, chip, core]).astype(jnp.int32)
    router = router_weight.T
    first, packed = pl.pallas_call(
        functools.partial(route_kernel, experts),
        out_shape=[shape((tokens_here, half), BF16), shape((tokens_here, half + LANES), BF16)],
        in_specs=[pl.BlockSpec(memory_space=pltpu.HBM)] * 4,
        out_specs=[pl.BlockSpec(memory_space=pltpu.VMEM)] * 2,
        scratch_shapes=[
            pltpu.VMEM(expert_ids.shape[::-1], jnp.int32),
            pltpu.VMEM((tokens_here, width), BF16),
            pltpu.VMEM((experts, width), BF16),
            pltpu.VMEM((tokens_here, width), BF16),
            pltpu.SemaphoreType.DMA((4,)),
        ],
        compiler_params=pltpu.CompilerParams(vmem_limit_bytes=VMEM_BYTES),
        cost_estimate=pl.CostEstimate(flops=0, bytes_accessed=0, transcendentals=0),
        name="route",
    )(*in_hbm(expert_ids.T, normed, router, upstream))
    if n_expert == 4:
        first_1, second_2 = over_expert(first, 1), over_expert(packed, 2)
        second_1, first_2 = over_expert(packed, 1), over_expert(first, 2)
        firsts = [first, first_1, first_2, over_expert(first_1, 2)]
        seconds = [packed, second_1, second_2, over_expert(second_2, 1)]
    else:
        firsts = [first] + [over_expert(first, k) for k in range(1, n_expert)]
        seconds = [packed] + [over_expert(packed, k) for k in range(1, n_expert)]

    blocks = n_dp if even else 8
    sources = [jnp.transpose(saved_inputs[0], (0, 2, 1, 3)).reshape(exp_dev * capacity, n_expert, width)]
    sources += [jnp.transpose(w, (1, 0, 2)) for w in (gate_weight, up_weight, down_weight)]
    results = (
        [shape((slots, width), BF16)]
        + [shape((hidden_all, width), BF16)] * 3
        + [shape((slots, hidden_all), F32)] * 2
    )
    inputs, gate, up, down, pre_gate, pre_up = pl.pallas_call(
        functools.partial(prepare_kernel, blocks),
        out_shape=results,
        in_specs=[pl.BlockSpec(memory_space=pltpu.HBM)] * 4,
        out_specs=[pl.BlockSpec(memory_space=pltpu.VMEM)] * len(results),
        scratch_shapes=[pltpu.VMEM(source.shape, BF16) for source in sources]
        + [pltpu.SemaphoreType.DMA((4 * blocks,))],
        compiler_params=pltpu.CompilerParams(vmem_limit_bytes=VMEM_BYTES),
        cost_estimate=pl.CostEstimate(flops=0, bytes_accessed=0, transcendentals=0),
        name="prepare",
    )(*in_hbm(*sources))

    outs = call(
        functools.partial(expert_kernel, (n_expert, exp_dev, capacity, tokens_here)),
        "experts",
        [shape((tokens_here, LANES), F32)] * n_expert
        + [shape((tokens, slots), BF16)]
        + [shape((slots, hidden_all), BF16)] * 3
        + [shape((tokens, width), BF16)],
        (at, *firsts, *seconds, down, pre_gate, pre_up),
        scalars=True,
    )
    scores, by_slot, arrived = outs[:n_expert], outs[n_expert:-1], outs[-1]
    back_scores = [scores[0]] + [over_expert(scores[k], k) for k in range(1, n_expert)]
    tok_gate, tok_up, *turned = call(
        functools.partial(core_kernel, (n_expert, exp_dev, n_chip, piece, even)),
        "core_terms",
        [shape((tokens, hidden_all), BF16)] * 2
        + [shape((hidden_all, slots), BF16)] * 2
        + [shape((hidden_all, tokens), BF16)]
        + [shape((n_chip, 3 * hidden_all, piece), BF16)] * even,
        (at, *seconds, *by_slot, arrived, inputs),
        scalars=True,
    )
    turned, theirs = turned[:3], turned[3:]
    if even:
        from_core = over_core(theirs[0])
        (mine,) = call(
            functools.partial(weight_kernel, (n_chip, piece)),
            "weight_terms",
            [shape((n_chip, 3 * hidden_all, piece), F32)],
            (at, arrived, inputs, *turned),
            scalars=True,
        )
    if even:
        chip_sums = call(
            add_kernel,
            "core_sum",
            [shape((3 * hidden_all, piece), BF16 if k else F32) for k in range(n_chip)],
            (mine, from_core),
        )
    else:
        terms = [dot(turned[0], inputs, (1, 0)), dot(turned[1], inputs, (1, 0)), dot(turned[2], arrived, (1, 0))]
        terms = jnp.concatenate(terms, axis=0).reshape(3 * hidden_all, n_chip, 2, piece)
        terms = jnp.transpose(terms, (2, 1, 0, 3))
        from_core = over_core(terms[1 - core].astype(BF16))
        terms = terms[core] + from_core.astype(F32)
        chip_sums = [terms[chip ^ k].astype(BF16 if k else F32) for k in range(n_chip)]
    chip_sums, back_scores = lax.optimization_barrier((chip_sums, back_scores))
    moved = {k: over_chip(chip_sums[k], k) for k in range(n_chip - 1, 1, -1)}

    always = dp < n_dp

    def add_terms(terms, dtype, *behind):
        kernel = functools.partial(terms_kernel, len(terms))
        return call(kernel, "add_terms", [shape(terms[0].shape, dtype)], (*terms, *behind), behind=len(behind))[0]

    def add_pair(total, move, k, dtype=BF16):
        return add_terms([total, move(total, 1 << k)], dtype)

    expert_rounds, chip_rounds = n_expert.bit_length() - 1, n_chip.bit_length() - 1

    def sum_chips(values):
        total, near = values
        for k in range(chip_rounds - 1):
            total = add_pair(total, over_chip, k)
            if k == 0:
                near, total = lax.optimization_barrier((near, total))
        last = over_chip(total, 1 << (chip_rounds - 1))
        return over_chip(near, 1), (total, last), (over_core(total), over_core(last))

    def as_one(function, values):
        outs = jax.eval_shape(function, values)
        return lax.cond(always, function, lambda values: jax.tree.map(lambda o: jnp.zeros(o.shape, o.dtype), outs), values)

    def way_back(values):
        back_scores, packed, normed, router, tok_gate, tok_up, gate, up, near = values
        other, own, through = call(
            functools.partial(router_kernel, experts, n_expert),
            "router_terms",
            [shape((experts, half), F32)] * 2 + [shape((tokens_here, width), F32)],
            (at, *back_scores, packed, normed, router),
            scalars=True,
        )
        (row_pieces,) = call(
            functools.partial(row_kernel, n_expert, 8),
            "row_terms",
            [shape((n_expert, tokens_here, width), BF16)],
            (at, tok_gate, tok_up, gate, up, other),
            scalars=True,
            behind=1,
        )
        total = add_terms([own, over_core(other)], BF16)
        if n_expert == 4:
            total = add_terms([total] + [over_expert(total, k) for k in range(1, n_expert)], BF16)
        else:
            for k in range(expert_rounds):
                total = add_pair(total, over_expert, k)
        row_pieces, total = lax.optimization_barrier((row_pieces, total))
        back_rows = lax.all_to_all(row_pieces, "expert", 0, 0, tiled=True)
        return *as_one(sum_chips, (total, near)), through, back_rows

    near, mine, theirs, *back = as_one(way_back, (back_scores, packed, normed, router, tok_gate, tok_up, gate, up, chip_sums[1]))
    chip_pieces = [chip_sums[0], near] + [moved[k] for k in range(2, n_chip)]
    grad_normed, router_grad, *grads = call(
        functools.partial(finish_kernel, (exp_dev, hidden_units)),
        "finish",
        [shape((tokens_here, width), BF16), shape((experts, width), F32)]
        + [shape((hidden_units, exp_dev, piece), F32)] * 3,
        (at, *chip_pieces, *mine, *theirs, *back),
        scalars=True,
    )
    grads = [jnp.transpose(g, (1, 0, 2)) for g in grads]
    return (grad_normed, router_grad.T, *grads)


def solution(mesh):
    placed = (
        P(("dp", "expert"), None),
        P(("dp", "expert"), None),
        P(("dp", "expert"), None),
        P(),
        P("expert", None, None),
        P("expert", None, None),
        P("expert", None, None),
        P("dp", "expert", None, None, None),
    )
    return jax.shard_map(
        on_device,
        mesh=mesh,
        in_specs=placed,
        out_specs=(
            P(("dp", "expert"), None),
            P(),
            P("expert", None, "dp"),
            P("expert", None, "dp"),
            P("expert", None, "dp"),
        ),
        check_vma=False,
    )
```

```python
import functools

import jax
import jax.numpy as jnp
from jax import lax
from jax.experimental import pallas as pl
from jax.experimental.pallas import tpu as pltpu
from jax.sharding import PartitionSpec as P

F32 = jnp.float32
BF16 = jnp.bfloat16
LANES = 128
VMEM_BYTES = 16 * 2**20


def dot(left, right, contract):
    return lax.dot_general(
        left,
        right,
        ((contract[:1], contract[1:]), ((), ())),
        preferred_element_type=F32,
    )


def iota(shape, dim):
    return lax.broadcasted_iota(jnp.int32, shape, dim)


def split_high_low(value):
    high = value.astype(BF16)
    return high, (value - high.astype(F32)).astype(BF16)


def route_kernel(experts, *refs):
    sources, (first, packed, ids, normed, router, upstream, sems) = refs[:4], refs[4:]
    tokens, width = normed.shape
    half = width // 2
    copies = [
        pltpu.make_async_copy(source, target, sems.at[k])
        for k, (source, target) in enumerate(zip(sources, (ids, normed, router, upstream)))
    ]
    for copy in copies:
        copy.start()
    copies[0].wait()
    expert = iota((experts, tokens), 0)
    named_t = expert < 0
    for k in range(ids.shape[0]):
        named_t = named_t | (ids[k : k + 1, :] == expert)
    unit = (iota((tokens, tokens), 0) == iota((tokens, tokens), 1)).astype(F32).astype(BF16)
    named_f = dot(unit, named_t.astype(F32).astype(BF16), (1, 1))
    named = named_f > 0.5
    earlier = (iota((tokens, tokens), 1) < iota((tokens, tokens), 0)).astype(F32).astype(BF16)
    slot = dot(earlier, named_f.astype(BF16), (1, 0))
    code = jnp.where(named, slot + 1.0, 0.0)
    copies[1].wait()
    copies[2].wait()
    logits = dot(normed[...], router[...], (1, 1))
    largest = jnp.max(jnp.where(named, logits, -jnp.inf), axis=1, keepdims=True)
    weight = jnp.where(named, jnp.exp(jnp.where(named, logits - largest, 0.0)), 0.0)
    weight = weight / jnp.sum(weight, axis=1, keepdims=True)
    high = weight.astype(BF16).astype(F32)
    middle = (weight - high).astype(BF16).astype(F32)
    low = weight - high - middle
    rest = jnp.zeros((tokens, LANES - 4 * experts), F32)
    packed[:, half:] = jnp.concatenate([high, middle, low, code, rest], axis=1).astype(BF16)
    copies[3].wait()
    first[...] = upstream[:, :half]
    packed[:, :half] = upstream[:, half:]


def prepare_kernel(blocks, *refs):
    sources, refs = refs[:4], refs[4:]
    scratch, sems, refs = refs[-5:-1], refs[-1], refs[:-5]
    inputs, gate_rows, up_rows, down_rows, pre_gate, pre_up = refs
    step = inputs.shape[1] // blocks
    copies = []
    for j in range(blocks):
        lanes = pl.ds(j * step, step)
        for k in range(4):
            copy = pltpu.make_async_copy(sources[k].at[:, :, lanes], scratch[k].at[:, :, lanes], sems.at[4 * j + k])
            copy.start()
            copies.append(copy)
    pre_gate[...] = jnp.zeros_like(pre_gate)
    pre_up[...] = jnp.zeros_like(pre_up)
    for j in range(blocks):
        lanes = slice(j * step, (j + 1) * step)
        for k, target in enumerate((inputs, gate_rows, up_rows, down_rows)):
            copies[4 * j + k].wait()
            target[:, lanes] = scratch[k][:, :, lanes].reshape(target.shape[0], step)
        pre_gate[...] += dot(inputs[:, lanes], gate_rows[:, lanes], (1, 1))
        pre_up[...] += dot(inputs[:, lanes], up_rows[:, lanes], (1, 1))


def pick(expert_of_column, experts, groups, columns):
    lane = iota((LANES, columns), 0)
    out = lane < 0
    for g in groups:
        out = out | (lane == expert_of_column + g * experts)
    return out.astype(F32).astype(BF16)


def block_terms(turned, inputs, arrived, start, piece):
    gate, up, hidden = turned
    at = pl.ds(pl.multiple_of(start, LANES), piece)
    return [dot(gate, inputs[:, at], (1, 0)), dot(up, inputs[:, at], (1, 0)), dot(hidden, arrived[:, at], (1, 0))]


def expert_kernel(sizes, at, *refs):
    n_expert, exp_dev, capacity, tokens_here = sizes
    firsts, seconds, rest = refs[:n_expert], refs[n_expert : 2 * n_expert], refs[2 * n_expert :]
    down, pre_gate, pre_up = rest[:3]
    scores = rest[3 : 3 + n_expert]
    place, slot_gate, slot_up, slot_hidden, arrived = rest[3 + n_expert :]
    me = at[0]
    experts = exp_dev * n_expert
    tokens = tokens_here * n_expert
    hidden_all, width = down.shape
    half = width // 2
    slots = exp_dev * capacity * n_expert
    packed = jnp.concatenate([u[:, half:] for u in seconds], axis=0)
    for r in range(n_expert):
        rows = slice(r * tokens_here, (r + 1) * tokens_here)
        arrived[rows, :half] = firsts[r][...]
        arrived[rows, half:] = seconds[r][:, :half]
    grad_hidden_raw = dot(arrived[...], down[...], (1, 1))

    expert_of_hidden = me * exp_dev + iota((LANES, hidden_all), 1) % exp_dev
    weight_hidden = dot(packed, pick(expert_of_hidden, experts, (0, 1, 2), hidden_all), (1, 0))
    expert_of_slot = me * exp_dev + iota((LANES, slots), 1) // (capacity * n_expert)
    code_at = dot(packed, pick(expert_of_slot, experts, (3,), slots), (1, 0))
    column = iota((tokens, slots), 1)
    source = me ^ (iota((tokens, slots), 0) // tokens_here)
    slot_code = ((column // n_expert) % capacity + 1).astype(F32)
    chosen = (source == column % n_expert) & (jnp.abs(code_at - slot_code) < 0.5)
    placed = chosen.astype(F32).astype(BF16)
    place[...] = placed

    high, low = split_high_low(grad_hidden_raw * weight_hidden)
    grad_hidden = dot(placed, high, (0, 0)) + dot(placed, low, (0, 0))
    same = iota((slots, hidden_all), 1) % exp_dev == iota((slots, hidden_all), 0) // (capacity * n_expert)
    v = pre_gate[...]
    logistic = jax.nn.sigmoid(v)
    activated = v * logistic
    hidden = jnp.where(same, activated * pre_up[...], 0.0).astype(BF16)
    slope = logistic * (1.0 + v * (1.0 - logistic))
    slot_hidden[...] = hidden
    slot_gate[...] = jnp.where(same, grad_hidden * pre_up[...] * slope, 0.0).astype(BF16)
    slot_up[...] = jnp.where(same, grad_hidden * activated, 0.0).astype(BF16)
    score = jnp.sum(hidden.astype(F32) * grad_hidden, axis=1, keepdims=True)
    expert_of_row = me * exp_dev + iota((slots, LANES), 0) // (capacity * n_expert)
    score = jnp.where(iota((slots, LANES), 1) == expert_of_row, score, 0.0)
    high, low = split_high_low(score)
    picked = dot(placed, high, (1, 0)) + dot(placed, low, (1, 0))
    for r in range(n_expert):
        scores[r][...] = picked[r * tokens_here : (r + 1) * tokens_here]


def core_kernel(sizes, at, *refs):
    n_expert, exp_dev, n_chip, piece, even = sizes
    seconds, rest = refs[:n_expert], refs[n_expert:]
    place, slot_gate, slot_up, slot_hidden, arrived, inputs = rest[:6]
    tok_gate, tok_up, turned_gate, turned_up, turned_hidden = rest[6:11]
    me, chip, core = at[0], at[1], at[2]
    experts = exp_dev * n_expert
    hidden_all = slot_gate.shape[1]
    hidden_units = hidden_all // exp_dev
    half = arrived.shape[1] // 2
    packed = jnp.concatenate([u[:, half:] for u in seconds], axis=0)
    expert_of_hidden = me * exp_dev + iota((LANES, hidden_all), 1) % exp_dev
    weight_hidden = dot(packed, pick(expert_of_hidden, experts, (0, 1, 2), hidden_all), (1, 0))
    scaled_hidden = (dot(place[...], slot_hidden[...], (1, 0)) * weight_hidden).astype(BF16)
    row, column = iota((hidden_all, hidden_all), 0), iota((hidden_all, hidden_all), 1)
    order = row == (column % exp_dev) * hidden_units + column // exp_dev
    order = order.astype(F32).astype(BF16)
    turned = [dot(order, value, (1, 1)).astype(BF16) for value in (slot_gate[...], slot_up[...], scaled_hidden)]
    turned_gate[...], turned_up[...], turned_hidden[...] = turned
    if even:
        theirs = rest[11]
        for r in range(n_chip):
            terms = block_terms(turned, inputs, arrived, (2 * (chip ^ r) + 1 - core) * piece, piece)
            for k in range(3):
                theirs[r, k * hidden_all : (k + 1) * hidden_all] = terms[k].astype(BF16)
    tok_gate[...] = dot(place[...], slot_gate[...], (1, 0)).astype(BF16)
    tok_up[...] = dot(place[...], slot_up[...], (1, 0)).astype(BF16)


def weight_kernel(sizes, at, arrived, inputs, gate, up, hidden, mine):
    n_chip, piece = sizes
    chip, core = at[1], at[2]
    n = gate.shape[0]
    for r in range(n_chip):
        start = (2 * (chip ^ r) + core) * piece
        terms = block_terms((gate[...], up[...], hidden[...]), inputs, arrived, start, piece)
        for k in range(3):
            mine[r, k * n : (k + 1) * n] = terms[k]


def add_kernel(mine, theirs, *outs):
    for r in range(len(outs)):
        outs[r][...] = (mine[r] + theirs[r].astype(F32)).astype(outs[r].dtype)


def row_kernel(n_expert, blocks, at, tok_gate, tok_up, gate, up, grad_logits, router, out):
    high, low = split_high_low(grad_logits[...])
    size = tok_gate.shape[0] // n_expert
    step = gate.shape[1] // blocks
    for j in range(blocks):
        lanes = slice(j * step, (j + 1) * step)
        total = dot(tok_gate[...], gate[:, lanes], (1, 0)) + dot(tok_up[...], up[:, lanes], (1, 0))
        through = dot(high, router[:, lanes], (1, 0)) + dot(low, router[:, lanes], (1, 0))
        for r in range(n_expert):
            piece = total[r * size : (r + 1) * size]
            out[at[0] ^ r, :, lanes] = (piece if r else piece + through).astype(out.dtype)


def router_kernel(experts, n_expert, at, *refs):
    scores, (packed, normed, other, own, kept) = refs[:n_expert], refs[n_expert:]
    picked = scores[0][...]
    for s in scores[1:]:
        picked = picked + s[...]
    picked = picked[:, :experts]
    half = normed.shape[1] // 2
    tail = packed[:, half:].astype(F32)
    weight = tail[:, :experts] + tail[:, experts : 2 * experts] + tail[:, 2 * experts : 3 * experts]
    code = tail[:, 3 * experts : 4 * experts]
    grad = jnp.where(code > 0.5, picked - weight * jnp.sum(picked, axis=1, keepdims=True), 0.0)
    high, low = split_high_low(grad)
    core = at[2]
    for out, part in ((other, 1 - core), (own, core)):
        values = normed[:, pl.ds(pl.multiple_of(part * half, LANES), half)]
        out[...] = dot(high, values, (0, 0)) + dot(low, values, (0, 0))
    kept[...] = grad


def terms_kernel(count, *refs):
    terms, out = refs[:count], refs[-1]
    while len(terms) > 1:
        terms = [terms[k][...].astype(F32) + terms[k + 1][...].astype(F32) for k in range(0, len(terms), 2)]
    out[...] = terms[0].astype(out.dtype)


def finish_kernel(sizes, at, *refs):
    exp_dev, hidden_units = sizes
    pieces, halves, back = refs[:-10], refs[-10:-6], refs[-6]
    grad_normed, router_grad, *outs = refs[-5:]
    core = at[2]
    half = halves[0].shape[1]
    for k in range(2):
        lanes = pl.ds(pl.multiple_of((core ^ k) * half, LANES), half)
        router_grad[:, lanes] = halves[2 * k][...].astype(F32) + halves[2 * k + 1][...].astype(F32)
    rows_total = back[0].astype(F32)
    for r in range(1, back.shape[0]):
        rows_total = rows_total + back[r].astype(F32)
    grad_normed[...] = rows_total.astype(grad_normed.dtype)
    total = pieces[0][...]
    for piece in pieces[1:]:
        total = total + piece[...].astype(F32)
    for k in range(3):
        for e in range(exp_dev):
            first = (k * exp_dev + e) * hidden_units
            outs[k][:, e, :] = total[first : first + hidden_units]


def on_device(normed, upstream, expert_ids, router_weight, gate_weight, up_weight, down_weight, saved_inputs):
    n_expert = lax.axis_size("expert")
    n_dp = lax.axis_size("dp")
    n_chip = n_dp // 2
    me = lax.axis_index("expert")
    dp = lax.axis_index("dp")
    core = dp & 1
    chip = dp >> 1
    exp_dev, hidden_units, width = gate_weight.shape
    capacity = saved_inputs.shape[3]
    experts = exp_dev * n_expert
    tokens_here = normed.shape[0]
    tokens = tokens_here * n_expert
    slots = exp_dev * capacity * n_expert
    hidden_all = exp_dev * hidden_units
    piece = width // n_dp
    half = width // 2
    even = piece % LANES == 0
    shape = jax.ShapeDtypeStruct

    def over_expert(value, k):
        return lax.ppermute(value, "expert", [(i, i ^ k) for i in range(n_expert)])

    def over_core(value):
        return lax.ppermute(value, "dp", [(i, i ^ 1) for i in range(n_dp)])

    def over_chip(value, k):
        return lax.ppermute(value, "dp", [(i, i ^ (2 * k)) for i in range(n_dp)])

    def in_hbm(*values):
        return [pltpu.with_memory_space_constraint(value, pltpu.HBM) for value in values]

    def call(kernel, name, outs, args, scalars=False, behind=0):
        specs = [pl.BlockSpec(memory_space=pltpu.VMEM)] * len(args)
        if scalars:
            specs[0] = pl.BlockSpec(memory_space=pltpu.SMEM)
        for k in range(behind):
            specs[-1 - k] = pl.BlockSpec(memory_space=pl.ANY)
        return pl.pallas_call(
            kernel,
            out_shape=outs,
            in_specs=specs,
            out_specs=[pl.BlockSpec(memory_space=pltpu.VMEM)] * len(outs),
            compiler_params=pltpu.CompilerParams(vmem_limit_bytes=VMEM_BYTES),
            cost_estimate=pl.CostEstimate(flops=0, bytes_accessed=0, transcendentals=0),
            name=name,
        )(*args)

    at = jnp.stack([me, chip, core]).astype(jnp.int32)
    router = router_weight.T
    first, packed = pl.pallas_call(
        functools.partial(route_kernel, experts),
        out_shape=[shape((tokens_here, half), BF16), shape((tokens_here, half + LANES), BF16)],
        in_specs=[pl.BlockSpec(memory_space=pltpu.HBM)] * 4,
        out_specs=[pl.BlockSpec(memory_space=pltpu.VMEM)] * 2,
        scratch_shapes=[
            pltpu.VMEM(expert_ids.shape[::-1], jnp.int32),
            pltpu.VMEM((tokens_here, width), BF16),
            pltpu.VMEM((experts, width), BF16),
            pltpu.VMEM((tokens_here, width), BF16),
            pltpu.SemaphoreType.DMA((4,)),
        ],
        compiler_params=pltpu.CompilerParams(vmem_limit_bytes=VMEM_BYTES),
        cost_estimate=pl.CostEstimate(flops=0, bytes_accessed=0, transcendentals=0),
        name="route",
    )(*in_hbm(expert_ids.T, normed, router, upstream))
    if n_expert == 4:
        first_1, second_2 = over_expert(first, 1), over_expert(packed, 2)
        second_1, first_2 = over_expert(packed, 1), over_expert(first, 2)
        firsts = [first, first_1, first_2, over_expert(first_1, 2)]
        seconds = [packed, second_1, second_2, over_expert(second_2, 1)]
    else:
        firsts = [first] + [over_expert(first, k) for k in range(1, n_expert)]
        seconds = [packed] + [over_expert(packed, k) for k in range(1, n_expert)]

    blocks = n_dp if even else 8
    sources = [jnp.transpose(saved_inputs[0], (0, 2, 1, 3)).reshape(exp_dev * capacity, n_expert, width)]
    sources += [jnp.transpose(w, (1, 0, 2)) for w in (gate_weight, up_weight, down_weight)]
    results = (
        [shape((slots, width), BF16)]
        + [shape((hidden_all, width), BF16)] * 3
        + [shape((slots, hidden_all), F32)] * 2
    )
    inputs, gate, up, down, pre_gate, pre_up = pl.pallas_call(
        functools.partial(prepare_kernel, blocks),
        out_shape=results,
        in_specs=[pl.BlockSpec(memory_space=pltpu.HBM)] * 4,
        out_specs=[pl.BlockSpec(memory_space=pltpu.VMEM)] * len(results),
        scratch_shapes=[pltpu.VMEM(source.shape, BF16) for source in sources]
        + [pltpu.SemaphoreType.DMA((4 * blocks,))],
        compiler_params=pltpu.CompilerParams(vmem_limit_bytes=VMEM_BYTES),
        cost_estimate=pl.CostEstimate(flops=0, bytes_accessed=0, transcendentals=0),
        name="prepare",
    )(*in_hbm(*sources))

    outs = call(
        functools.partial(expert_kernel, (n_expert, exp_dev, capacity, tokens_here)),
        "experts",
        [shape((tokens_here, LANES), F32)] * n_expert
        + [shape((tokens, slots), BF16)]
        + [shape((slots, hidden_all), BF16)] * 3
        + [shape((tokens, width), BF16)],
        (at, *firsts, *seconds, down, pre_gate, pre_up),
        scalars=True,
    )
    scores, by_slot, arrived = outs[:n_expert], outs[n_expert:-1], outs[-1]
    back_scores = [scores[0]] + [over_expert(scores[k], k) for k in range(1, n_expert)]
    tok_gate, tok_up, *turned = call(
        functools.partial(core_kernel, (n_expert, exp_dev, n_chip, piece, even)),
        "core_terms",
        [shape((tokens, hidden_all), BF16)] * 2
        + [shape((hidden_all, slots), BF16)] * 2
        + [shape((hidden_all, tokens), BF16)]
        + [shape((n_chip, 3 * hidden_all, piece), BF16)] * even,
        (at, *seconds, *by_slot, arrived, inputs),
        scalars=True,
    )
    turned, theirs = turned[:3], turned[3:]
    if even:
        from_core = over_core(theirs[0])
        (mine,) = call(
            functools.partial(weight_kernel, (n_chip, piece)),
            "weight_terms",
            [shape((n_chip, 3 * hidden_all, piece), F32)],
            (at, arrived, inputs, *turned),
            scalars=True,
        )
    if even:
        chip_sums = call(
            add_kernel,
            "core_sum",
            [shape((3 * hidden_all, piece), BF16 if k else F32) for k in range(n_chip)],
            (mine, from_core),
        )
    else:
        terms = [dot(turned[0], inputs, (1, 0)), dot(turned[1], inputs, (1, 0)), dot(turned[2], arrived, (1, 0))]
        terms = jnp.concatenate(terms, axis=0).reshape(3 * hidden_all, n_chip, 2, piece)
        terms = jnp.transpose(terms, (2, 1, 0, 3))
        from_core = over_core(terms[1 - core].astype(BF16))
        terms = terms[core] + from_core.astype(F32)
        chip_sums = [terms[chip ^ k].astype(BF16 if k else F32) for k in range(n_chip)]
    chip_sums, back_scores = lax.optimization_barrier((chip_sums, back_scores))
    moved = {k: over_chip(chip_sums[k], k) for k in range(n_chip - 1, 1, -1)}

    always = dp < n_dp

    def add_terms(terms, dtype, *behind):
        kernel = functools.partial(terms_kernel, len(terms))
        return call(kernel, "add_terms", [shape(terms[0].shape, dtype)], (*terms, *behind), behind=len(behind))[0]

    def add_pair(total, move, k, dtype=BF16):
        return add_terms([total, move(total, 1 << k)], dtype)

    expert_rounds, chip_rounds = n_expert.bit_length() - 1, n_chip.bit_length() - 1

    def sum_chips(values):
        total, near = values
        for k in range(chip_rounds - 1):
            total = add_pair(total, over_chip, k)
            if k == 0:
                near, total = lax.optimization_barrier((near, total))
        last = over_chip(total, 1 << (chip_rounds - 1))
        return over_chip(near, 1), (total, last), (over_core(total), over_core(last))

    def as_one(function, values):
        outs = jax.eval_shape(function, values)
        return lax.cond(always, function, lambda values: jax.tree.map(lambda o: jnp.zeros(o.shape, o.dtype), outs), values)

    def way_back(values):
        back_scores, packed, normed, router, tok_gate, tok_up, gate, up, near = values
        other, own, grad_logits = call(
            functools.partial(router_kernel, experts, n_expert),
            "router_terms",
            [shape((experts, half), F32)] * 2 + [shape((tokens_here, experts), F32)],
            (at, *back_scores, packed, normed),
            scalars=True,
        )
        (row_pieces,) = call(
            functools.partial(row_kernel, n_expert, 8),
            "row_terms",
            [shape((n_expert, tokens_here, width), BF16)],
            (at, tok_gate, tok_up, gate, up, grad_logits, router),
            scalars=True,
        )
        total = add_terms([own, over_core(other)], BF16)
        if n_expert == 4:
            total = add_terms([total] + [over_expert(total, k) for k in range(1, n_expert)], BF16)
        else:
            for k in range(expert_rounds):
                total = add_pair(total, over_expert, k)
        row_pieces, total = lax.optimization_barrier((row_pieces, total))
        back_rows = lax.all_to_all(row_pieces, "expert", 0, 0, tiled=True)
        return *as_one(sum_chips, (total, near)), back_rows

    near, mine, theirs, *back = as_one(way_back, (back_scores, packed, normed, router, tok_gate, tok_up, gate, up, chip_sums[1]))
    chip_pieces = [chip_sums[0], near] + [moved[k] for k in range(2, n_chip)]
    grad_normed, router_grad, *grads = call(
        functools.partial(finish_kernel, (exp_dev, hidden_units)),
        "finish",
        [shape((tokens_here, width), BF16), shape((experts, width), F32)]
        + [shape((hidden_units, exp_dev, piece), F32)] * 3,
        (at, *chip_pieces, *mine, *theirs, *back),
        scalars=True,
    )
    grads = [jnp.transpose(g, (1, 0, 2)) for g in grads]
    return (grad_normed, router_grad.T, *grads)


def solution(mesh):
    placed = (
        P(("dp", "expert"), None),
        P(("dp", "expert"), None),
        P(("dp", "expert"), None),
        P(),
        P("expert", None, None),
        P("expert", None, None),
        P("expert", None, None),
        P("dp", "expert", None, None, None),
    )
    return jax.shard_map(
        on_device,
        mesh=mesh,
        in_specs=placed,
        out_specs=(
            P(("dp", "expert"), None),
            P(),
            P("expert", None, "dp"),
            P("expert", None, "dp"),
            P("expert", None, "dp"),
        ),
        check_vma=False,
    )
```

```python
import functools

import jax
import jax.numpy as jnp
from jax import lax
from jax.experimental import pallas as pl
from jax.experimental.pallas import tpu as pltpu
from jax.sharding import PartitionSpec as P

F32 = jnp.float32
BF16 = jnp.bfloat16
LANES = 128
VMEM_BYTES = 16 * 2**20


def dot(left, right, contract):
    return lax.dot_general(
        left,
        right,
        ((contract[:1], contract[1:]), ((), ())),
        preferred_element_type=F32,
    )


def iota(shape, dim):
    return lax.broadcasted_iota(jnp.int32, shape, dim)


def split_high_low(value):
    high = value.astype(BF16)
    return high, (value - high.astype(F32)).astype(BF16)


def route_kernel(experts, *refs):
    sources, (first, packed, ids, normed, router, upstream, sems) = refs[:4], refs[4:]
    tokens, width = normed.shape
    half = width // 2
    copies = [
        pltpu.make_async_copy(source, target, sems.at[k])
        for k, (source, target) in enumerate(zip(sources, (ids, normed, router, upstream)))
    ]
    for copy in copies:
        copy.start()
    copies[0].wait()
    expert = iota((experts, tokens), 0)
    named_t = expert < 0
    for k in range(ids.shape[0]):
        named_t = named_t | (ids[k : k + 1, :] == expert)
    unit = (iota((tokens, tokens), 0) == iota((tokens, tokens), 1)).astype(F32).astype(BF16)
    named_f = dot(unit, named_t.astype(F32).astype(BF16), (1, 1))
    named = named_f > 0.5
    earlier = (iota((tokens, tokens), 1) < iota((tokens, tokens), 0)).astype(F32).astype(BF16)
    slot = dot(earlier, named_f.astype(BF16), (1, 0))
    code = jnp.where(named, slot + 1.0, 0.0)
    copies[1].wait()
    copies[2].wait()
    logits = dot(normed[...], router[...], (1, 1))
    largest = jnp.max(jnp.where(named, logits, -jnp.inf), axis=1, keepdims=True)
    weight = jnp.where(named, jnp.exp(jnp.where(named, logits - largest, 0.0)), 0.0)
    weight = weight / jnp.sum(weight, axis=1, keepdims=True)
    high = weight.astype(BF16).astype(F32)
    middle = (weight - high).astype(BF16).astype(F32)
    low = weight - high - middle
    rest = jnp.zeros((tokens, LANES - 4 * experts), F32)
    packed[:, half:] = jnp.concatenate([high, middle, low, code, rest], axis=1).astype(BF16)
    copies[3].wait()
    first[...] = upstream[:, :half]
    packed[:, :half] = upstream[:, half:]


def prepare_kernel(blocks, *refs):
    sources, refs = refs[:4], refs[4:]
    scratch, sems, refs = refs[-5:-1], refs[-1], refs[:-5]
    inputs, gate_rows, up_rows, down_rows, pre_gate, pre_up = refs
    step = inputs.shape[1] // blocks
    copies = []
    for j in range(blocks):
        lanes = pl.ds(j * step, step)
        for k in range(4):
            copy = pltpu.make_async_copy(sources[k].at[:, :, lanes], scratch[k].at[:, :, lanes], sems.at[4 * j + k])
            copy.start()
            copies.append(copy)
    pre_gate[...] = jnp.zeros_like(pre_gate)
    pre_up[...] = jnp.zeros_like(pre_up)
    for j in range(blocks):
        lanes = slice(j * step, (j + 1) * step)
        for k, target in enumerate((inputs, gate_rows, up_rows, down_rows)):
            copies[4 * j + k].wait()
            target[:, lanes] = scratch[k][:, :, lanes].reshape(target.shape[0], step)
        pre_gate[...] += dot(inputs[:, lanes], gate_rows[:, lanes], (1, 1))
        pre_up[...] += dot(inputs[:, lanes], up_rows[:, lanes], (1, 1))


def pick(expert_of_column, experts, groups, columns):
    lane = iota((LANES, columns), 0)
    out = lane < 0
    for g in groups:
        out = out | (lane == expert_of_column + g * experts)
    return out.astype(F32).astype(BF16)


def block_terms(turned, inputs, arrived, start, piece):
    gate, up, hidden = turned
    at = pl.ds(pl.multiple_of(start, LANES), piece)
    return [dot(gate, inputs[:, at], (1, 0)), dot(up, inputs[:, at], (1, 0)), dot(hidden, arrived[:, at], (1, 0))]


def expert_kernel(sizes, at, *refs):
    n_expert, exp_dev, capacity, tokens_here = sizes
    firsts, seconds, rest = refs[:n_expert], refs[n_expert : 2 * n_expert], refs[2 * n_expert :]
    down, pre_gate, pre_up = rest[:3]
    scores = rest[3 : 3 + n_expert]
    place, slot_gate, slot_up, slot_hidden, arrived = rest[3 + n_expert :]
    me = at[0]
    experts = exp_dev * n_expert
    tokens = tokens_here * n_expert
    hidden_all, width = down.shape
    half = width // 2
    slots = exp_dev * capacity * n_expert
    packed = jnp.concatenate([u[:, half:] for u in seconds], axis=0)
    for r in range(n_expert):
        rows = slice(r * tokens_here, (r + 1) * tokens_here)
        arrived[rows, :half] = firsts[r][...]
        arrived[rows, half:] = seconds[r][:, :half]
    grad_hidden_raw = dot(arrived[...], down[...], (1, 1))

    expert_of_hidden = me * exp_dev + iota((LANES, hidden_all), 1) % exp_dev
    weight_hidden = dot(packed, pick(expert_of_hidden, experts, (0, 1, 2), hidden_all), (1, 0))
    expert_of_slot = me * exp_dev + iota((LANES, slots), 1) // (capacity * n_expert)
    code_at = dot(packed, pick(expert_of_slot, experts, (3,), slots), (1, 0))
    column = iota((tokens, slots), 1)
    source = me ^ (iota((tokens, slots), 0) // tokens_here)
    slot_code = ((column // n_expert) % capacity + 1).astype(F32)
    chosen = (source == column % n_expert) & (jnp.abs(code_at - slot_code) < 0.5)
    placed = chosen.astype(F32).astype(BF16)
    place[...] = placed

    high, low = split_high_low(grad_hidden_raw * weight_hidden)
    grad_hidden = dot(placed, high, (0, 0)) + dot(placed, low, (0, 0))
    same = iota((slots, hidden_all), 1) % exp_dev == iota((slots, hidden_all), 0) // (capacity * n_expert)
    v = pre_gate[...]
    logistic = jax.nn.sigmoid(v)
    activated = v * logistic
    hidden = jnp.where(same, activated * pre_up[...], 0.0).astype(BF16)
    slope = logistic * (1.0 + v * (1.0 - logistic))
    slot_hidden[...] = hidden
    slot_gate[...] = jnp.where(same, grad_hidden * pre_up[...] * slope, 0.0).astype(BF16)
    slot_up[...] = jnp.where(same, grad_hidden * activated, 0.0).astype(BF16)
    score = jnp.sum(hidden.astype(F32) * grad_hidden, axis=1, keepdims=True)
    expert_of_row = me * exp_dev + iota((slots, LANES), 0) // (capacity * n_expert)
    score = jnp.where(iota((slots, LANES), 1) == expert_of_row, score, 0.0)
    high, low = split_high_low(score)
    picked = dot(placed, high, (1, 0)) + dot(placed, low, (1, 0))
    for r in range(n_expert):
        scores[r][...] = picked[r * tokens_here : (r + 1) * tokens_here]


def core_kernel(sizes, at, *refs):
    n_expert, exp_dev, n_chip, piece, even = sizes
    seconds, rest = refs[:n_expert], refs[n_expert:]
    place, slot_gate, slot_up, slot_hidden, arrived, inputs = rest[:6]
    tok_gate, tok_up, turned_gate, turned_up, turned_hidden = rest[6:11]
    me, chip, core = at[0], at[1], at[2]
    experts = exp_dev * n_expert
    hidden_all = slot_gate.shape[1]
    hidden_units = hidden_all // exp_dev
    half = arrived.shape[1] // 2
    packed = jnp.concatenate([u[:, half:] for u in seconds], axis=0)
    expert_of_hidden = me * exp_dev + iota((LANES, hidden_all), 1) % exp_dev
    weight_hidden = dot(packed, pick(expert_of_hidden, experts, (0, 1, 2), hidden_all), (1, 0))
    scaled_hidden = (dot(place[...], slot_hidden[...], (1, 0)) * weight_hidden).astype(BF16)
    row, column = iota((hidden_all, hidden_all), 0), iota((hidden_all, hidden_all), 1)
    order = row == (column % exp_dev) * hidden_units + column // exp_dev
    order = order.astype(F32).astype(BF16)
    turned = [dot(order, value, (1, 1)).astype(BF16) for value in (slot_gate[...], slot_up[...], scaled_hidden)]
    turned_gate[...], turned_up[...], turned_hidden[...] = turned
    if even:
        theirs = rest[11]
        for r in range(n_chip):
            terms = block_terms(turned, inputs, arrived, (2 * (chip ^ r) + 1 - core) * piece, piece)
            for k in range(3):
                theirs[r, k * hidden_all : (k + 1) * hidden_all] = terms[k].astype(BF16)
    tok_gate[...] = dot(place[...], slot_gate[...], (1, 0)).astype(BF16)
    tok_up[...] = dot(place[...], slot_up[...], (1, 0)).astype(BF16)


def weight_kernel(sizes, at, arrived, inputs, gate, up, hidden, mine):
    n_chip, piece = sizes
    chip, core = at[1], at[2]
    n = gate.shape[0]
    for r in range(n_chip):
        start = (2 * (chip ^ r) + core) * piece
        terms = block_terms((gate[...], up[...], hidden[...]), inputs, arrived, start, piece)
        for k in range(3):
            mine[r, k * n : (k + 1) * n] = terms[k]


def add_kernel(mine, theirs, *outs):
    for r in range(len(outs)):
        outs[r][...] = (mine[r] + theirs[r].astype(F32)).astype(outs[r].dtype)


def row_kernel(n_expert, blocks, at, tok_gate, tok_up, gate, up, grad_logits, router, out):
    high, low = split_high_low(grad_logits[...])
    size = tok_gate.shape[0] // n_expert
    step = gate.shape[1] // blocks
    for j in range(blocks):
        lanes = slice(j * step, (j + 1) * step)
        total = dot(tok_gate[...], gate[:, lanes], (1, 0)) + dot(tok_up[...], up[:, lanes], (1, 0))
        through = dot(high, router[:, lanes], (1, 0)) + dot(low, router[:, lanes], (1, 0))
        for r in range(n_expert):
            piece = total[r * size : (r + 1) * size]
            out[at[0] ^ r, :, lanes] = (piece if r else piece + through).astype(out.dtype)


def router_kernel(experts, n_expert, at, *refs):
    scores, (packed, normed, other, own, kept) = refs[:n_expert], refs[n_expert:]
    picked = scores[0][...]
    for s in scores[1:]:
        picked = picked + s[...]
    picked = picked[:, :experts]
    half = normed.shape[1] // 2
    tail = packed[:, half:].astype(F32)
    weight = tail[:, :experts] + tail[:, experts : 2 * experts] + tail[:, 2 * experts : 3 * experts]
    code = tail[:, 3 * experts : 4 * experts]
    grad = jnp.where(code > 0.5, picked - weight * jnp.sum(picked, axis=1, keepdims=True), 0.0)
    high, low = split_high_low(grad)
    core = at[2]
    for out, part in ((other, 1 - core), (own, core)):
        values = normed[:, pl.ds(pl.multiple_of(part * half, LANES), half)]
        out[...] = dot(high, values, (0, 0)) + dot(low, values, (0, 0))
    kept[...] = grad


def terms_kernel(count, *refs):
    terms, out = refs[:count], refs[-1]
    while len(terms) > 1:
        terms = [terms[k][...].astype(F32) + terms[k + 1][...].astype(F32) for k in range(0, len(terms), 2)]
    out[...] = terms[0].astype(out.dtype)


def finish_kernel(sizes, at, *refs):
    exp_dev, hidden_units = sizes
    pieces, halves, back = refs[:-10], refs[-10:-6], refs[-6]
    grad_normed, router_grad, *outs = refs[-5:]
    core = at[2]
    half = halves[0].shape[1]
    for k in range(2):
        lanes = pl.ds(pl.multiple_of((core ^ k) * half, LANES), half)
        router_grad[:, lanes] = halves[2 * k][...].astype(F32) + halves[2 * k + 1][...].astype(F32)
    rows_total = back[0].astype(F32)
    for r in range(1, back.shape[0]):
        rows_total = rows_total + back[r].astype(F32)
    grad_normed[...] = rows_total.astype(grad_normed.dtype)
    total = pieces[0][...]
    for piece in pieces[1:]:
        total = total + piece[...].astype(F32)
    for k in range(3):
        for e in range(exp_dev):
            first = (k * exp_dev + e) * hidden_units
            outs[k][:, e, :] = total[first : first + hidden_units]


def on_device(normed, upstream, expert_ids, router_weight, gate_weight, up_weight, down_weight, saved_inputs):
    n_expert = lax.axis_size("expert")
    n_dp = lax.axis_size("dp")
    n_chip = n_dp // 2
    me = lax.axis_index("expert")
    dp = lax.axis_index("dp")
    core = dp & 1
    chip = dp >> 1
    exp_dev, hidden_units, width = gate_weight.shape
    capacity = saved_inputs.shape[3]
    experts = exp_dev * n_expert
    tokens_here = normed.shape[0]
    tokens = tokens_here * n_expert
    slots = exp_dev * capacity * n_expert
    hidden_all = exp_dev * hidden_units
    piece = width // n_dp
    half = width // 2
    even = piece % LANES == 0
    shape = jax.ShapeDtypeStruct

    def over_expert(value, k):
        return lax.ppermute(value, "expert", [(i, i ^ k) for i in range(n_expert)])

    def over_core(value):
        return lax.ppermute(value, "dp", [(i, i ^ 1) for i in range(n_dp)])

    def over_chip(value, k):
        return lax.ppermute(value, "dp", [(i, i ^ (2 * k)) for i in range(n_dp)])

    def in_hbm(*values):
        return [pltpu.with_memory_space_constraint(value, pltpu.HBM) for value in values]

    def call(kernel, name, outs, args, scalars=False, behind=0):
        specs = [pl.BlockSpec(memory_space=pltpu.VMEM)] * len(args)
        if scalars:
            specs[0] = pl.BlockSpec(memory_space=pltpu.SMEM)
        for k in range(behind):
            specs[-1 - k] = pl.BlockSpec(memory_space=pl.ANY)
        return pl.pallas_call(
            kernel,
            out_shape=outs,
            in_specs=specs,
            out_specs=[pl.BlockSpec(memory_space=pltpu.VMEM)] * len(outs),
            compiler_params=pltpu.CompilerParams(vmem_limit_bytes=VMEM_BYTES),
            cost_estimate=pl.CostEstimate(flops=0, bytes_accessed=0, transcendentals=0),
            name=name,
        )(*args)

    at = jnp.stack([me, chip, core]).astype(jnp.int32)
    router = router_weight.T
    first, packed = pl.pallas_call(
        functools.partial(route_kernel, experts),
        out_shape=[shape((tokens_here, half), BF16), shape((tokens_here, half + LANES), BF16)],
        in_specs=[pl.BlockSpec(memory_space=pltpu.HBM)] * 4,
        out_specs=[pl.BlockSpec(memory_space=pltpu.VMEM)] * 2,
        scratch_shapes=[
            pltpu.VMEM(expert_ids.shape[::-1], jnp.int32),
            pltpu.VMEM((tokens_here, width), BF16),
            pltpu.VMEM((experts, width), BF16),
            pltpu.VMEM((tokens_here, width), BF16),
            pltpu.SemaphoreType.DMA((4,)),
        ],
        compiler_params=pltpu.CompilerParams(vmem_limit_bytes=VMEM_BYTES),
        cost_estimate=pl.CostEstimate(flops=0, bytes_accessed=0, transcendentals=0),
        name="route",
    )(*in_hbm(expert_ids.T, normed, router, upstream))
    if n_expert == 4:
        first_1, second_2 = over_expert(first, 1), over_expert(packed, 2)
        second_1, first_2 = over_expert(packed, 1), over_expert(first, 2)
        firsts = [first, first_1, first_2, over_expert(first_1, 2)]
        seconds = [packed, second_1, second_2, over_expert(second_2, 1)]
    else:
        firsts = [first] + [over_expert(first, k) for k in range(1, n_expert)]
        seconds = [packed] + [over_expert(packed, k) for k in range(1, n_expert)]

    blocks = n_dp if even else 8
    sources = [jnp.transpose(saved_inputs[0], (0, 2, 1, 3)).reshape(exp_dev * capacity, n_expert, width)]
    sources += [jnp.transpose(w, (1, 0, 2)) for w in (gate_weight, up_weight, down_weight)]
    results = (
        [shape((slots, width), BF16)]
        + [shape((hidden_all, width), BF16)] * 3
        + [shape((slots, hidden_all), F32)] * 2
    )
    inputs, gate, up, down, pre_gate, pre_up = pl.pallas_call(
        functools.partial(prepare_kernel, blocks),
        out_shape=results,
        in_specs=[pl.BlockSpec(memory_space=pltpu.HBM)] * 4,
        out_specs=[pl.BlockSpec(memory_space=pltpu.VMEM)] * len(results),
        scratch_shapes=[pltpu.VMEM(source.shape, BF16) for source in sources]
        + [pltpu.SemaphoreType.DMA((4 * blocks,))],
        compiler_params=pltpu.CompilerParams(vmem_limit_bytes=VMEM_BYTES),
        cost_estimate=pl.CostEstimate(flops=0, bytes_accessed=0, transcendentals=0),
        name="prepare",
    )(*in_hbm(*sources))

    outs = call(
        functools.partial(expert_kernel, (n_expert, exp_dev, capacity, tokens_here)),
        "experts",
        [shape((tokens_here, LANES), F32)] * n_expert
        + [shape((tokens, slots), BF16)]
        + [shape((slots, hidden_all), BF16)] * 3
        + [shape((tokens, width), BF16)],
        (at, *firsts, *seconds, down, pre_gate, pre_up),
        scalars=True,
    )
    scores, by_slot, arrived = outs[:n_expert], outs[n_expert:-1], outs[-1]
    back_scores = [scores[0]] + [over_expert(scores[k], k) for k in range(1, n_expert)]
    tok_gate, tok_up, *turned = call(
        functools.partial(core_kernel, (n_expert, exp_dev, n_chip, piece, even)),
        "core_terms",
        [shape((tokens, hidden_all), BF16)] * 2
        + [shape((hidden_all, slots), BF16)] * 2
        + [shape((hidden_all, tokens), BF16)]
        + [shape((n_chip, 3 * hidden_all, piece), BF16)] * even,
        (at, *seconds, *by_slot, arrived, inputs),
        scalars=True,
    )
    turned, theirs = turned[:3], turned[3:]
    if even:
        from_core = over_core(theirs[0])
        (mine,) = call(
            functools.partial(weight_kernel, (n_chip, piece)),
            "weight_terms",
            [shape((n_chip, 3 * hidden_all, piece), F32)],
            (at, arrived, inputs, *turned),
            scalars=True,
        )
    if even:
        chip_sums = call(
            add_kernel,
            "core_sum",
            [shape((3 * hidden_all, piece), BF16 if k else F32) for k in range(n_chip)],
            (mine, from_core),
        )
    else:
        terms = [dot(turned[0], inputs, (1, 0)), dot(turned[1], inputs, (1, 0)), dot(turned[2], arrived, (1, 0))]
        terms = jnp.concatenate(terms, axis=0).reshape(3 * hidden_all, n_chip, 2, piece)
        terms = jnp.transpose(terms, (2, 1, 0, 3))
        from_core = over_core(terms[1 - core].astype(BF16))
        terms = terms[core] + from_core.astype(F32)
        chip_sums = [terms[chip ^ k].astype(BF16 if k else F32) for k in range(n_chip)]
    chip_sums, back_scores = lax.optimization_barrier((chip_sums, back_scores))
    moved = {k: over_chip(chip_sums[k], k) for k in range(n_chip - 1, 1, -1)}

    always = dp < n_dp

    def add_terms(terms, dtype, *behind):
        kernel = functools.partial(terms_kernel, len(terms))
        return call(kernel, "add_terms", [shape(terms[0].shape, dtype)], (*terms, *behind), behind=len(behind))[0]

    def add_pair(total, move, k, dtype=BF16):
        return add_terms([total, move(total, 1 << k)], dtype)

    expert_rounds, chip_rounds = n_expert.bit_length() - 1, n_chip.bit_length() - 1

    def sum_chips(values):
        total, near = values
        for k in range(chip_rounds - 1):
            partner = over_chip(total, 1 << k)
            if k == 0:
                near, partner = lax.optimization_barrier((near, partner))
            total = add_terms([total, partner], BF16)
        last = over_chip(total, 1 << (chip_rounds - 1))
        return over_chip(near, 1), (total, last), (over_core(total), over_core(last))

    def as_one(function, values):
        outs = jax.eval_shape(function, values)
        return lax.cond(always, function, lambda values: jax.tree.map(lambda o: jnp.zeros(o.shape, o.dtype), outs), values)

    def way_back(values):
        back_scores, packed, normed, router, tok_gate, tok_up, gate, up, near = values
        other, own, grad_logits = call(
            functools.partial(router_kernel, experts, n_expert),
            "router_terms",
            [shape((experts, half), F32)] * 2 + [shape((tokens_here, experts), F32)],
            (at, *back_scores, packed, normed),
            scalars=True,
        )
        (row_pieces,) = call(
            functools.partial(row_kernel, n_expert, 8),
            "row_terms",
            [shape((n_expert, tokens_here, width), BF16)],
            (at, tok_gate, tok_up, gate, up, grad_logits, router),
            scalars=True,
        )
        total = add_terms([own, over_core(other)], BF16)
        if n_expert == 4:
            total = add_terms([total] + [over_expert(total, k) for k in range(1, n_expert)], BF16)
        else:
            for k in range(expert_rounds):
                total = add_pair(total, over_expert, k)
        row_pieces, total = lax.optimization_barrier((row_pieces, total))
        back_rows = lax.all_to_all(row_pieces, "expert", 0, 0, tiled=True)
        return *as_one(sum_chips, (total, near)), back_rows

    near, mine, theirs, *back = as_one(way_back, (back_scores, packed, normed, router, tok_gate, tok_up, gate, up, chip_sums[1]))
    chip_pieces = [chip_sums[0], near] + [moved[k] for k in range(2, n_chip)]
    grad_normed, router_grad, *grads = call(
        functools.partial(finish_kernel, (exp_dev, hidden_units)),
        "finish",
        [shape((tokens_here, width), BF16), shape((experts, width), F32)]
        + [shape((hidden_units, exp_dev, piece), F32)] * 3,
        (at, *chip_pieces, *mine, *theirs, *back),
        scalars=True,
    )
    grads = [jnp.transpose(g, (1, 0, 2)) for g in grads]
    return (grad_normed, router_grad.T, *grads)


def solution(mesh):
    placed = (
        P(("dp", "expert"), None),
        P(("dp", "expert"), None),
        P(("dp", "expert"), None),
        P(),
        P("expert", None, None),
        P("expert", None, None),
        P("expert", None, None),
        P("dp", "expert", None, None, None),
    )
    return jax.shard_map(
        on_device,
        mesh=mesh,
        in_specs=placed,
        out_specs=(
            P(("dp", "expert"), None),
            P(),
            P("expert", None, "dp"),
            P("expert", None, "dp"),
            P("expert", None, "dp"),
        ),
        check_vma=False,
    )
```
